256 devices in a mesh: attn: 32 (over z, y_lo, core), sect: 8 (over y_hi, x).
Axes of the slice: x: 4, y: 4 (y_hi: 2, y_lo: 2; y = y_hi * 2 + y_lo), z: 8, core: 2. Of those that a mesh axis runs over, the one named last changes fastest.
Arguments:
- queries: bfloat16 [512, 6144], P('attn', 'sect'), may hold values from -405 to 405
- stream: bfloat16 [512, 6144], P('attn', 'sect'), may hold values from -41 to 41
- kv_pool: bfloat16 [10240, 8, 16, 256], P('attn', 'sect'), may hold values from -6 to 6
- fresh_kv: bfloat16 [1024, 8, 16, 256], P('attn', 'sect'), may hold values from -6 to 6
- fresh_owner: int32 [1024, 1], P('attn'), may hold values from 0 to 31; in each aligned block of 32 rows (0 to 31, 32 to 63, ...) at most 4 rows name the same one
- page_table: int32 [512, 16], P('attn'), may hold values from 0 to 319
- lengths: int32 [32, 16], P('attn'), may hold values from 1 to 256, 2560 in all within a row
- norm_gain: bfloat16 [6144], P('sect'), may hold values from 0.25 to 1.75
- router: bfloat16 [6144, 4], P('sect'), may hold values from -0.078125 to 0.078125
- expert_ids: int32 [512, 2], P('attn'), may hold values from 0 to 3, all different within a row; in each aligned block of 16 rows (0 to 15, 16 to 31, ...) at most 10 rows name the same one
- w_gate: bfloat16 [6144, 32768], P(None, ('attn', 'sect')), may hold values from -0.078125 to 0.078125
- w_up: bfloat16 [6144, 32768], P(None, ('attn', 'sect')), may hold values from -0.078125 to 0.078125
- w_down: bfloat16 [32768, 6144], P(('attn', 'sect')), may hold values from -0.0625 to 0.0625
Outputs:
- mixed: bfloat16 [512, 6144], P('attn', 'sect')
- kv_out: bfloat16 [10240, 8, 16, 256], P('attn', 'sect')
The draws below stay inside these ranges and needn't reach their ends.
Inputs may be any that keep to these rules, and one draw needn't show every extreme that they name: `fresh_owner`: within each aligned block of 32 pages no owner is named more than 4 times, a bound that some block reaches. Each row of lengths sums to 2560, and its largest entry is 256. `expert_ids`: the two experts of a row differ. Within each aligned block of 16 rows no expert is named more than 10 times, a bound that some block reaches.
All inputs are finite; a program needn't handle non-finite values.
Results may differ from the reference program's by a relative error of at most 0.0052.
Values may be sent and summed in bfloat16 or wider, within the bound.
No kernel may reach another device: no remote copies, remote signals or barrier semaphores. Data moves between devices by JAX's collectives and lax.ppermute only.
A program may use at most 128 MiB of HBM per device.

```python
import math
import jax
import jax.numpy as jnp
import numpy as np
from jax import lax

D = 6144
HEADS = 48
KV_HEADS = 8
HD = 128
EXPERTS = 4
FFW = 8192
TOP = 2
PAGE = 16
PAGES_ROW = 16
CAPP = 4
ROWS_G = 16
OLD_PAGES = 192
NEW_DEV = 32
CAP = 10
CTX = 256
POOL = 320
ROWS_T = 512
N_ATTN = 32


def draw_queries(key, part):
    key = jax.random.fold_in(key, 11)
    base = jnp.clip(jax.random.normal(jax.random.fold_in(key, 1), (ROWS_T, HEADS * HD), jnp.float32), -4.5, 4.5)
    return base.astype(jnp.bfloat16)


def draw_stream(key, part):
    key = jax.random.fold_in(key, 23)
    row_scale = jnp.exp(jax.random.uniform(jax.random.fold_in(key, 1), (ROWS_T, 1), jnp.float32, jnp.log(0.3), jnp.log(3.0)))
    col_scale = jnp.exp(jax.random.uniform(jax.random.fold_in(key, 2), (1, D), jnp.float32, jnp.log(0.3), jnp.log(3.0)))
    base = jnp.clip(jax.random.normal(jax.random.fold_in(key, 3), (ROWS_T, D), jnp.float32), -4.5, 4.5)
    return (base * row_scale * col_scale).astype(jnp.bfloat16)


def touch_ends(values, key, smallest, top_value):
    spot = [jax.random.randint(jax.random.fold_in(key, axis), (), 0, length) for axis, length in enumerate(values.shape)]
    main_axis = values.shape.index(max(values.shape))
    next_to = spot[:main_axis] + [(spot[main_axis] + 1) % values.shape[main_axis]] + spot[main_axis + 1:]
    return values.at[tuple(spot)].set(smallest).at[tuple(next_to)].set(top_value)


def levels(rng, dims, shards, smallest, high):
    gain = 1.0
    for axis_at, shards_of in shards:
        draws = jax.random.uniform(jax.random.fold_in(jax.random.fold_in(rng, 6), axis_at), (shards_of,), jnp.float32, smallest / len(shards), high / len(shards))
        gain = gain * jnp.repeat(jnp.exp(draws), dims[axis_at] // shards_of).reshape((-1,) + (1,) * (len(dims) - 1 - axis_at))
    return gain


def profile(count, total, reach, lean):
    weights = [(1 << 20) // math.isqrt(standing ** lean) + 1 for standing in range(2, count + 1)]
    spare, given = total - reach - (count - 1), [1] * (count - 1)
    while spare > 0:
        candidates = [i for i in range(count - 1) if given[i] < reach]
        whole, remaining = sum([weights[i] for i in candidates]), spare
        for i in candidates:
            extra = min(reach - given[i], max(1, remaining * weights[i] // whole), spare)
            given[i] = given[i] + extra
            spare = spare - extra
    return np.array([reach] + given)


def ragged(stream_key, amount, total, limit, slope):
    if amount == 2:
        one = jax.random.randint(stream_key, (), max(1, total - limit), min(limit, total - 1) + 1)
        return jnp.stack([one, total - one])
    tallies = jnp.asarray(profile(amount, total, limit, slope), jnp.int32)
    pairs = (amount - 1) // 2
    source_of, taker = tallies[1:1 + 2 * pairs:2], tallies[2:2 + 2 * pairs:2]
    room = jnp.minimum(source_of - 1, limit - taker)
    shifted = jax.random.randint(jax.random.fold_in(stream_key, 1), (pairs,), 0, 1 << 20) % (room + 1)
    tallies = tallies.at[1:1 + 2 * pairs:2].set(source_of - shifted).at[2:2 + 2 * pairs:2].set(taker + shifted)
    return tallies[jax.random.permutation(jax.random.fold_in(stream_key, 2), amount)]


def routed_block(key, own, number, rows, number_of, top, reach, slope):
    order = jax.random.permutation(key, number_of)
    crowded, usual = shares(number_of, rows * top, reach, slope, True), shares(number_of, rows * top, reach, slope, False)
    places = jnp.arange(number_of)

    def named(sizes, rotation):
        used = int((sizes > 0).sum())
        fixed = max(1, used // 4)
        moved = fixed + (places - fixed + rotation * (used - fixed)) % max(1, number_of - fixed)
        return jnp.zeros((number_of,), jnp.int32).at[order[jnp.where(places < fixed, places, moved)]].set(jnp.asarray(sizes, jnp.int32))

    sizes = jnp.where(number % 4 == 0, named(crowded, number // 4), named(usual, number - number // 4 - 1))
    mixed = jax.random.permutation(jax.random.fold_in(own, 3), number_of)
    source_of, sink = mixed[0:number_of // 2 * 2:2], mixed[1:number_of // 2 * 2:2]
    room = jnp.minimum(sizes[source_of] - 1, reach - sizes[sink]) // 2
    room = jnp.where((source_of == order[0]) | (sink == order[0]) | (sizes[sink] == 0), 0, jnp.maximum(room, 0))
    moved = jax.random.randint(jax.random.fold_in(own, 4), (number_of // 2,), 0, 1 << 20) % (room + 1)
    sizes = sizes.at[source_of].add(-moved).at[sink].add(moved)
    items = jnp.searchsorted(jnp.cumsum(sizes), jnp.arange(rows * top), side="right").astype(jnp.int32)
    table = items.reshape(top, rows).T
    table = table[jax.random.permutation(jax.random.fold_in(own, 1), rows)]
    rotation = jax.random.randint(jax.random.fold_in(own, 2), (rows, 1), 0, top)
    return jnp.take_along_axis(table, (jnp.arange(top)[None, :] + rotation) % top, axis=1)


def shares(count, total, limit, skew, full):
    loads = [(1 << 20) // math.isqrt(standing ** skew) + 1 for standing in range(1, count + 1)]
    largest = limit if full else min(limit, max(-(-total // count), total * loads[0] // sum(loads)))
    least = 1 if total - largest >= count - 1 else 0
    given, rest = [largest] + [least] * (count - 1), total - largest - least * (count - 1)
    while rest > 0:
        movable = [i for i in range(1, count) if given[i] < largest] or [i for i in range(1, count) if given[i] < limit]
        whole, budget = sum([loads[i] for i in movable]), rest
        for i in movable:
            extra = min(limit - given[i], max(1, budget * loads[i] // whole), rest)
            given[i] = given[i] + extra
            rest = rest - extra
    return np.array(given)


def bell_draw(rng, extent, scale, bound, cuts=(), kind=jnp.bfloat16):
    values = scale * jax.random.normal(rng, extent, jnp.float32)
    if cuts:
        values = values * levels(rng, extent, cuts, -0.22, 0.18)
    return jnp.clip(values, -bound, bound).astype(kind)


def setup_inputs(seed: int = 0) -> dict:
    arg_keys = jax.random.split(jax.random.key(seed), 14)
    queries = draw_queries(jax.random.fold_in(arg_keys[13], 71), 0)
    stream = draw_stream(jax.random.fold_in(arg_keys[13], 71), 0)
    kv_pool = bell_draw(arg_keys[2], (N_ATTN * POOL, KV_HEADS, PAGE, 2 * HD), 1.0, 6.0, ((0, 32), (1, 8)))
    fresh_kv = bell_draw(arg_keys[3], (N_ATTN * NEW_DEV, KV_HEADS, PAGE, 2 * HD), 1.0, 6.0, ((0, 32), (1, 8)))
    fresh_owner_keys = jax.random.split(jax.random.fold_in(arg_keys[4], 1), (N_ATTN * NEW_DEV) // NEW_DEV)
    fresh_owner_turns = jax.random.permutation(jax.random.fold_in(arg_keys[4], 3), (N_ATTN * NEW_DEV) // NEW_DEV)
    fresh_owner = jax.vmap(lambda own, number: routed_block(jax.random.fold_in(arg_keys[4], 2), own, number, NEW_DEV, N_ATTN, 1, CAPP, 2))(fresh_owner_keys, fresh_owner_turns).reshape((N_ATTN * NEW_DEV, 1))
    page_table = touch_ends(jax.random.randint(arg_keys[5], (ROWS_T, PAGES_ROW), 0, POOL), jax.random.fold_in(arg_keys[5], 1), 0, POOL - 1).astype(jnp.int32)
    lengths = jax.vmap(lambda own: ragged(own, ROWS_G, ROWS_G * CTX * 5 // 8, CTX, 2))(jax.random.split(arg_keys[6], N_ATTN)).reshape((N_ATTN, ROWS_G)).astype(jnp.int32)
    norm_gain = jnp.clip(1.0 + 0.15 * jax.random.normal(arg_keys[7], (D,), jnp.float32), 0.25, 1.75).astype(jnp.bfloat16)
    router = bell_draw(arg_keys[8], (D, EXPERTS), D ** -0.5, 0.078125, ((0, 8),))
    expert_ids_keys = jax.random.split(jax.random.fold_in(arg_keys[9], 1), ROWS_T // ROWS_G)
    expert_ids_turns = jax.random.permutation(jax.random.fold_in(arg_keys[9], 3), ROWS_T // ROWS_G)
    expert_ids = jax.vmap(lambda own, number: routed_block(jax.random.fold_in(arg_keys[9], 2), own, number, ROWS_G, EXPERTS, 2, CAP, 1))(expert_ids_keys, expert_ids_turns).reshape((ROWS_T, TOP))
    w_gate = bell_draw(arg_keys[10], (D, EXPERTS * FFW), D ** -0.5, 0.078125, ((1, 256),))
    w_up = bell_draw(arg_keys[11], (D, EXPERTS * FFW), D ** -0.5, 0.078125, ((1, 256),))
    w_down = bell_draw(arg_keys[12], (EXPERTS * FFW, D), FFW ** -0.5, 0.0625, ((0, 256),))
    return dict(queries=queries, stream=stream, kv_pool=kv_pool, fresh_kv=fresh_kv, fresh_owner=fresh_owner, page_table=page_table, lengths=lengths, norm_gain=norm_gain, router=router, expert_ids=expert_ids, w_gate=w_gate, w_up=w_up, w_down=w_down)


def place_pages(kv_pool, fresh_kv, fresh_owner):
    owners = fresh_owner[:, 0].reshape(N_ATTN, NEW_DEV)
    owner_hot = (owners[:, :, None] == jnp.arange(N_ATTN, dtype=jnp.int32)[None, None, :]).astype(jnp.int32)
    earlier = jnp.cumsum(owner_hot, axis=1) - owner_hot
    place = lax.optimization_barrier(jnp.sum(earlier * owner_hot, axis=2))
    region_slot = (jnp.arange(N_ATTN, dtype=jnp.int32)[:, None] * CAPP + place).astype(jnp.int32)
    page_shape = fresh_kv.shape[1:]
    region = jnp.zeros((N_ATTN, N_ATTN * CAPP) + page_shape, fresh_kv.dtype)
    region = region.at[owners, region_slot].set(fresh_kv.reshape((N_ATTN, NEW_DEV) + page_shape))
    kept = kv_pool.reshape((N_ATTN, POOL) + page_shape)[:, :OLD_PAGES]
    return jnp.concatenate([kept, region], axis=1)

def attend(block):
    query, pages, table, length = block
    fetched = pages[table]
    keys = fetched[..., :HD].astype(jnp.float32)
    values = fetched[..., HD:].astype(jnp.float32)
    grouped = query.reshape(ROWS_G, KV_HEADS, HEADS // KV_HEADS, HD).astype(jnp.float32)
    scores = jnp.einsum('rkgd,rpksd->rkgps', grouped, keys) * float(HD) ** (-0.5)
    scores = scores.reshape(ROWS_G, KV_HEADS, HEADS // KV_HEADS, CTX)
    valid = (jnp.arange(CTX, dtype=jnp.int32)[None, :] < length[:, None])[:, None, None, :]
    masked = jnp.where(valid, scores, -1e+30)
    top = lax.optimization_barrier(jnp.max(masked, axis=-1, keepdims=True))
    weights = jnp.where(valid, jnp.exp(masked - top), 0.0)
    total = lax.optimization_barrier(jnp.sum(weights, axis=-1))
    rounded = weights.astype(jnp.bfloat16).astype(jnp.float32)
    rounded = rounded.reshape(ROWS_G, KV_HEADS, HEADS // KV_HEADS, PAGES_ROW, PAGE)
    summed = jnp.einsum('rkgps,rpksd->rkgd', rounded, values)
    return (summed / total[..., None]).reshape(ROWS_G, D)

def reference(queries, stream, kv_pool, fresh_kv, fresh_owner, page_table, lengths, norm_gain, router, expert_ids, w_gate, w_up, w_down):
    pool = place_pages(kv_pool, fresh_kv, fresh_owner)
    attended = lax.map(attend, (queries.reshape(N_ATTN, ROWS_G, HEADS * HD), pool, page_table.reshape(N_ATTN, ROWS_G, PAGES_ROW), lengths))
    attended = attended.reshape(ROWS_T, D)
    hidden = (stream.astype(jnp.float32) + attended).astype(jnp.bfloat16)
    hidden_f = hidden.astype(jnp.float32)
    inverse = lax.rsqrt(lax.optimization_barrier(jnp.sum(hidden_f * hidden_f, axis=1)) / D + 1e-05)
    normed = (hidden_f * inverse[:, None] * norm_gain.astype(jnp.float32)[None, :]).astype(jnp.bfloat16)
    logits = jnp.dot(normed, router, preferred_element_type=jnp.float32)
    chosen = expert_ids[:, :, None] == jnp.arange(EXPERTS, dtype=jnp.int32)[None, None, :]
    picked = lax.optimization_barrier(jnp.sum(jnp.where(chosen, logits[:, None, :], 0.0), axis=2))
    first = jax.nn.sigmoid(picked[:, 0] - picked[:, 1])
    second = jax.nn.sigmoid(picked[:, 1] - picked[:, 0])
    gate_by_expert = lax.optimization_barrier(jnp.sum(jnp.where(chosen, jnp.stack([first, second], axis=1)[:, :, None], 0.0), axis=1))
    routed = lax.optimization_barrier(jnp.sum(chosen.astype(jnp.int32), axis=1)).reshape(N_ATTN, ROWS_G, EXPERTS)
    slot = jnp.cumsum(routed, axis=1) - routed
    assign = (routed[..., None] == 1) & (slot[..., None] == jnp.arange(CAP, dtype=jnp.int32))
    packed = jnp.einsum('arec,ard->eacd', assign.astype(jnp.float32), normed.reshape(N_ATTN, ROWS_G, D).astype(jnp.float32)).astype(jnp.bfloat16)

    def run_expert(index):
        start = (index * FFW).astype(jnp.int32)
        gate_cols = lax.dynamic_slice_in_dim(w_gate, start, FFW, 1)
        up_cols = lax.dynamic_slice_in_dim(w_up, start, FFW, 1)
        down_rows = lax.dynamic_slice_in_dim(w_down, start, FFW, 0)
        rows_in = lax.dynamic_index_in_dim(packed, index, 0, keepdims=False).reshape(N_ATTN * CAP, D)
        gate_part = jnp.dot(rows_in, gate_cols, preferred_element_type=jnp.float32)
        up_part = jnp.dot(rows_in, up_cols, preferred_element_type=jnp.float32)
        active = (jax.nn.silu(gate_part) * up_part).astype(jnp.bfloat16)
        return jnp.dot(active, down_rows, preferred_element_type=jnp.float32)
    outputs = lax.map(run_expert, jnp.arange(EXPERTS, dtype=jnp.int32)).reshape(EXPERTS, N_ATTN, CAP, D)
    weighting = jnp.where(assign, gate_by_expert.reshape(N_ATTN, ROWS_G, EXPERTS)[..., None], 0.0)
    blended = jnp.einsum('arec,eacd->ard', weighting, outputs, precision=lax.Precision.HIGHEST).reshape(ROWS_T, D)
    mixed = (hidden_f + blended).astype(jnp.bfloat16)
    return (mixed, pool.reshape((N_ATTN * POOL,) + fresh_kv.shape[1:]))
```

```python
import functools

import jax
import jax.numpy as jnp
from jax import lax
from jax.experimental import pallas as pl
from jax.experimental.pallas import tpu as pltpu
from jax.sharding import PartitionSpec as P

F32 = jnp.float32
BF16 = jnp.bfloat16
EXPERTS = 4
CAPP = 4
OLD_PAGES = 192
CAP = 10
LANES = 128
SLAB = 64
SCALAR_ROW = 30
NZ = 8
ROWS = NZ * CAP
PIECES = 3
AXES = ("attn", "sect")
VMEM_BYTES = 56 * 1024 * 1024


def place(z, y, x, c):
    return (z * 4 + (y % 2) * 2 + c) * 8 + (y // 2) * 4 + x


def pairs(move):
    return [
        (place(z, y, x, c), place(*move(z, y, x, c)))
        for z in range(NZ)
        for y in range(4)
        for x in range(4)
        for c in range(2)
    ]


def along_x(step):
    return pairs(lambda z, y, x, c: (z, y, x ^ step, c))


def along_y(step):
    return pairs(lambda z, y, x, c: (z, y ^ step, x, c))


OTHER_CORE = pairs(lambda z, y, x, c: (z, y, x, c ^ 1))
Z_GROUPS = [[z * 4 + r for z in range(NZ)] for r in range(4)]


def permute(value, perm):
    return lax.ppermute(value, AXES, perm)


def gather4(value, along):
    return [value] + [permute(value, along(step)) for step in (1, 2, 3)]


def in_vmem(count):
    return [pl.BlockSpec(memory_space=pltpu.VMEM)] * count


def in_smem(count):
    return [pl.BlockSpec(memory_space=pltpu.SMEM)] * count


def params():
    return pltpu.CompilerParams(vmem_limit_bytes=VMEM_BYTES)


def iota(shape, dim):
    return lax.broadcasted_iota(jnp.int32, shape, dim)


def slab_offset(chunk):
    return jnp.where(chunk < 3, chunk * CAP, chunk * CAP + 2)


def pack_pages_kernel(owner, fresh, out, used):
    out[...] = jnp.zeros_like(out)

    def clear(o, carry):
        used[o] = 0
        return carry

    lax.fori_loop(0, used.shape[0], clear, 0)

    def put(p, carry):
        o = owner[p]
        k = used[o]
        out[o * CAPP + k] = fresh[p]
        used[o] = k + 1
        return carry

    lax.fori_loop(0, fresh.shape[0], put, 0, unroll=4)


def pack_pages(owners, fresh, n_attn):
    return pl.pallas_call(
        pack_pages_kernel,
        out_shape=jax.ShapeDtypeStruct((n_attn * CAPP,) + fresh.shape[1:], fresh.dtype),
        in_specs=in_smem(1) + in_vmem(1),
        out_specs=in_vmem(1)[0],
        scratch_shapes=[pltpu.SMEM((n_attn,), jnp.int32)],
        compiler_params=params(),
        name="pack_pages",
    )(owners, fresh)


def split3(value):
    pieces = []
    for _ in range(PIECES):
        piece = value.astype(BF16).astype(F32)
        pieces.append(piece)
        value = value - piece
    return pieces


def attend_kernel(
    table,
    lengths,
    queries,
    stream,
    kv_pool,
    arrived,
    gain,
    router,
    ids,
    kv_out,
    hidden_out,
    payload,
    select_out,
    pool,
    q_scr,
    o_scr,
    sems,
):
    rows, width = queries.shape
    heads = width // LANES
    pages = table.shape[1]
    load_old = pltpu.make_async_copy(
        kv_pool.at[pl.ds(0, OLD_PAGES)], pool.at[pl.ds(0, OLD_PAGES)], sems.at[0]
    )
    fresh_slots = pl.ds(OLD_PAGES, arrived.shape[0])
    load_new = pltpu.make_async_copy(arrived, pool.at[fresh_slots], sems.at[1])
    load_old.start()
    load_new.start()
    q_scr[...] = jnp.zeros_like(q_scr)
    for h in range(heads):
        q_scr[pl.ds(h, rows, stride=16), :] = queries[:, h * LANES : (h + 1) * LANES].astype(F32)

    ids_f = ids[...].astype(F32)
    cols = EXPERTS * 32
    spread = (iota((rows, cols), 1) % rows == iota((rows, cols), 0)).astype(F32)
    ids_l = lax.dot_general(ids_f, spread, (((0,), (0,)), ((), ())), preferred_element_type=F32)
    ids_l = ids_l.astype(jnp.int32)
    e0, e1 = ids_l[0:1], ids_l[1:2]
    expert = iota((8, cols), 0)
    routed = ((expert == e0) | (expert == e1)).astype(F32)
    before = ((iota((cols, cols), 0) < rows) & (iota((cols, cols), 0) < iota((cols, cols), 1) % rows)).astype(F32)
    slot = jnp.dot(routed, before, preferred_element_type=F32).astype(jnp.int32)
    slot0 = jnp.sum(jnp.where(expert == e0, slot, 0), axis=0, keepdims=True)
    slot1 = jnp.sum(jnp.where(expert == e1, slot, 0), axis=0, keepdims=True)
    column = iota((1, cols), 1)
    offset = slab_offset(column // rows)
    features = column < heads * rows
    target0 = jnp.where(
        features,
        e0 * SLAB + slot0 + offset,
        jnp.where(column < (heads + 1) * rows, e0 * SLAB + SCALAR_ROW, -1),
    )
    target1 = jnp.where(
        features,
        e1 * SLAB + slot1 + offset,
        jnp.where(column < (heads + 1) * rows, -1, e1 * SLAB + SCALAR_ROW),
    )
    at = iota((EXPERTS * SLAB, cols), 0)
    select = ((at == target0) | (at == target1)).astype(F32).astype(BF16)
    select_out[...] = select
    ids_c = ids[...]
    c0, c1 = ids_c[:, 0:1], ids_c[:, 1:2]
    expert_c = iota((rows, LANES), 1)
    routed_c = ((expert_c == c0) | (expert_c == c1)).astype(F32)
    before_c = (iota((rows, rows), 1) < iota((rows, rows), 0)).astype(F32)
    slot_c = jnp.dot(before_c, routed_c, preferred_element_type=F32).astype(jnp.int32)
    slot_c0 = jnp.sum(jnp.where(expert_c == c0, slot_c, 0), axis=1, keepdims=True)
    slot_c1 = jnp.sum(jnp.where(expert_c == c1, slot_c, 0), axis=1, keepdims=True)

    load_old.wait()
    load_new.wait()
    store = pltpu.make_async_copy(pool, kv_out, sems.at[2])
    store.start()
    scale = float(LANES) ** (-0.5)
    for r in range(rows):
        page_list = [pool[table[r, p]] for p in range(pages)]
        keys = jnp.concatenate([page[:, :LANES] for page in page_list], axis=0)
        values = jnp.concatenate([page[:, LANES:] for page in page_list], axis=0)
        query = q_scr[r * 16 : (r + 1) * 16, :].astype(BF16)
        scores = lax.dot_general(query, keys, (((1,), (1,)), ((), ())), preferred_element_type=F32)
        scores = scores[:8] * scale
        valid = iota(scores.shape, 1) < lengths[0, r]
        masked = jnp.where(valid, scores, -1e30)
        top = jnp.max(masked, axis=1, keepdims=True)
        weights = jnp.where(valid, jnp.exp(masked - top), 0.0)
        total = jnp.sum(weights, axis=1, keepdims=True)
        summed = jnp.dot(weights.astype(BF16), values, preferred_element_type=F32)
        o_scr[r * 8 : (r + 1) * 8, :] = summed / total
    attended = jnp.concatenate([o_scr[pl.ds(h, rows, stride=8), :] for h in range(heads)], axis=1)
    hidden = (stream[...].astype(F32) + attended).astype(BF16)
    hidden_out[...] = hidden
    hidden_f = hidden.astype(F32)
    squares = jnp.sum(hidden_f * hidden_f, axis=1, keepdims=True)
    gained = (hidden_f * gain[...].astype(F32)).astype(BF16)
    logits = jnp.dot(gained, router[...], preferred_element_type=F32)
    expert_r = iota(logits.shape, 1)
    delta = jnp.sum(
        jnp.where(expert_r == c0, logits, 0.0) - jnp.where(expert_r == c1, logits, 0.0),
        axis=1,
        keepdims=True,
    )
    lane = iota((rows, LANES), 1)

    def scalars(slots, difference):
        total = jnp.zeros((rows, LANES), F32)
        for i, piece in enumerate(split3(squares) + split3(difference)):
            total = total + jnp.where(lane == i * CAP + slots, piece, 0.0)
        return total.astype(BF16)

    parts = [gained[:, h * LANES : (h + 1) * LANES] for h in range(heads)]
    parts += [scalars(slot_c0, delta), scalars(slot_c1, -delta)]
    stacked = jnp.concatenate(parts, axis=0)
    slabs = jnp.dot(select, stacked, preferred_element_type=F32).astype(BF16)
    for e in range(EXPERTS):
        slab = slabs[e * SLAB : (e + 1) * SLAB]
        payload[2 * e] = slab
        payload[2 * e + 1] = slab
    store.wait()


def attend(table, lengths, queries, stream, kv_pool, arrived, gain, router, ids):
    rows, width = queries.shape
    anywhere = pl.BlockSpec(memory_space=pl.ANY)
    return pl.pallas_call(
        attend_kernel,
        out_shape=(
            jax.ShapeDtypeStruct(kv_pool.shape, kv_pool.dtype),
            jax.ShapeDtypeStruct((rows, width), BF16),
            jax.ShapeDtypeStruct((NZ, SLAB, LANES), BF16),
            jax.ShapeDtypeStruct((EXPERTS * SLAB, LANES), BF16),
        ),
        in_specs=in_smem(2) + in_vmem(2) + [anywhere, anywhere] + in_vmem(3),
        out_specs=tuple([anywhere] + in_vmem(3)),
        scratch_shapes=[
            pltpu.VMEM(kv_pool.shape, kv_pool.dtype),
            pltpu.VMEM((rows * 16, LANES), F32),
            pltpu.VMEM((rows * 8, LANES), F32),
            pltpu.SemaphoreType.DMA((3,)),
        ],
        compiler_params=params(),
        name="attend",
    )(table, lengths, queries, stream, kv_pool, arrived, gain, router, ids)


def to_rows_kernel(slabs, half_a, half_b):
    count = NZ * SLAB
    to, at = iota((count, count), 0), iota((count, count), 1)
    select = ((to % NZ) * SLAB + to // NZ == at).astype(F32).astype(BF16)
    flat = slabs[...].reshape(count, LANES)
    moved = jnp.dot(select, flat, preferred_element_type=F32).astype(BF16)
    half_a[...] = moved[: half_a.shape[0]]
    half_b[...] = moved[half_a.shape[0] : half_a.shape[0] + half_b.shape[0]]


def to_rows(slabs):
    return pl.pallas_call(
        to_rows_kernel,
        out_shape=(
            jax.ShapeDtypeStruct((3 * ROWS + 16, LANES), BF16),
            jax.ShapeDtypeStruct((3 * ROWS, LANES), BF16),
        ),
        in_specs=in_vmem(1),
        out_specs=tuple(in_vmem(2)),
        compiler_params=params(),
        name="to_rows",
    )(slabs)


def expert_kernel(where, *refs):
    a_refs = (refs[0:4], refs[4:8])
    b_refs = (refs[8:12], refs[12:16])
    w_gate, w_up, w_down = refs[16:19]
    out_a, out_b = (refs[19], refs[21]), (refs[20], refs[22])
    high, x = where[0], where[1]
    blocks = [(c, g) for c in range(2) for g in range(2)]
    width = 6 * LANES

    def section(hm, n):
        return jnp.bitwise_xor(high, hm) * 4 + jnp.bitwise_xor(x, n)

    def tile(c, m, n, chunk):
        if chunk < 3:
            start = n * (3 * ROWS + 16) + chunk * ROWS
            return a_refs[c][m][start : start + ROWS, :]
        start = m * 3 * ROWS + (chunk - 3) * ROWS
        return b_refs[c][n][start : start + ROWS, :]

    total = jnp.zeros((4 * ROWS, 2 * LANES), F32)
    for hm in range(2):
        for n in range(4):
            s = section(hm, n)
            for pair in range(3):
                left = jnp.concatenate(
                    [
                        jnp.concatenate(
                            [tile(c, 2 * hm + g, n, 2 * pair + i) for c, g in blocks], axis=0
                        )
                        for i in range(2)
                    ],
                    axis=1,
                )
                at = pl.ds(pl.multiple_of(s * width + pair * 2 * LANES, 2 * LANES), 2 * LANES)
                right = jnp.concatenate([w_gate[at, :], w_up[at, :]], axis=1)
                total = total + jnp.dot(left, right, preferred_element_type=F32)

    active = []
    for i, (c, g) in enumerate(blocks):
        sums = jnp.zeros((NZ, LANES), F32)
        for hm in range(2):
            for n in range(4):
                start = n * (3 * ROWS + 16) + 3 * ROWS
                sums = sums + a_refs[c][2 * hm + g][start : start + 16, :].astype(F32)[:NZ]

        def scalar(first):
            return sum(
                sums[:, (first + p) * CAP : (first + p + 1) * CAP] for p in range(PIECES)
            )

        inverse = lax.rsqrt(scalar(0) / (width * 8) + 1e-05)
        gate = 1.0 / (1.0 + jnp.exp(-scalar(PIECES) * inverse))
        part = total[i * ROWS : (i + 1) * ROWS]
        for k in range(CAP):
            rows = part[k * NZ : (k + 1) * NZ] * inverse[:, k : k + 1]
            v, up = rows[:, :LANES], rows[:, LANES:]
            active.append(v / (1.0 + jnp.exp(-v)) * up * gate[:, k : k + 1])
    active = jnp.concatenate(active, axis=0).astype(BF16)

    for hm in range(2):
        for n in range(4):
            s = section(hm, n)
            at = pl.ds(pl.multiple_of(s * width, width), width)
            made = jnp.dot(active, w_down[:, at], preferred_element_type=F32).astype(BF16)
            for i, (c, g) in enumerate(blocks):
                m = 2 * hm + g
                for chunk in range(6):
                    piece = made[i * ROWS : (i + 1) * ROWS, chunk * LANES : (chunk + 1) * LANES]
                    if chunk < 3:
                        out_a[c][n, m, chunk * ROWS : (chunk + 1) * ROWS, :] = piece
                    else:
                        out_b[c][m, n, (chunk - 3) * ROWS : (chunk - 2) * ROWS, :] = piece


def run_expert(where, own_a, other_a, own_b, other_b, w_gate, w_up, w_down):
    out = jax.ShapeDtypeStruct((4, 4, 3 * ROWS, LANES), BF16)
    return pl.pallas_call(
        expert_kernel,
        out_shape=(out,) * 4,
        in_specs=in_smem(1) + in_vmem(19),
        out_specs=tuple(in_vmem(4)),
        compiler_params=params(),
        name="expert",
    )(where, *own_a, *other_a, *own_b, *other_b, w_gate, w_up, w_down)


def add_cores_kernel(own_a, own_b, other_a, other_b, *outs):
    for n in range(4):
        outs[n][...] = (own_a[n].astype(F32) + other_a[n].astype(F32)).astype(BF16)
        outs[4 + n][...] = (own_b[n].astype(F32) + other_b[n].astype(F32)).astype(BF16)


def add_cores(own_a, own_b, other_a, other_b):
    out = jax.ShapeDtypeStruct(own_a.shape[1:], BF16)
    return pl.pallas_call(
        add_cores_kernel,
        out_shape=(out,) * 8,
        in_specs=in_vmem(4),
        out_specs=tuple(in_vmem(8)),
        compiler_params=params(),
        name="add_cores",
    )(own_a, own_b, other_a, other_b)


def sum4(refs):
    return (refs[0][...].astype(F32) + refs[1][...].astype(F32)) + (
        refs[2][...].astype(F32) + refs[3][...].astype(F32)
    )


def add_first_kernel(*refs):
    for half in range(2):
        summed = sum4(refs[4 * half : 4 * half + 4]).astype(BF16)
        for m in range(4):
            refs[8 + 4 * half + m][...] = summed[m]


def add_first(a, b):
    out = jax.ShapeDtypeStruct(a[0].shape[1:], BF16)
    return pl.pallas_call(
        add_first_kernel,
        out_shape=(out,) * 8,
        in_specs=in_vmem(8),
        out_specs=tuple(in_vmem(8)),
        compiler_params=params(),
        name="add_first",
    )(*a, *b)


def to_slabs_kernel(*refs):
    count = NZ * SLAB
    half = 3 * ROWS
    summed = jnp.concatenate([sum4(refs[0:4]), sum4(refs[4:8])], axis=0).astype(BF16)
    to, at = iota((count, 2 * half), 0), iota((count, 2 * half), 1)
    row = jnp.where(at < half, at // NZ, at // NZ + 2)
    select = ((at % NZ) * SLAB + row == to).astype(F32).astype(BF16)
    moved = jnp.dot(select, summed, preferred_element_type=F32).astype(BF16)
    refs[8][...] = moved.reshape(NZ, SLAB, LANES)


def to_slabs(a, b):
    return pl.pallas_call(
        to_slabs_kernel,
        out_shape=jax.ShapeDtypeStruct((NZ, SLAB, LANES), BF16),
        in_specs=in_vmem(8),
        out_specs=in_vmem(1)[0],
        compiler_params=params(),
        name="to_slabs",
    )(*a, *b)


def combine_kernel(slabs, hidden, select, mixed):
    rows, width = hidden.shape
    total = jnp.zeros((LANES, LANES), F32)
    for half in range(2):
        flat = jnp.concatenate([slabs[2 * e + half] for e in range(EXPERTS)], axis=0)
        total = total + lax.dot_general(
            select[...], flat, (((0,), (0,)), ((), ())), preferred_element_type=F32
        )
    blended = jnp.concatenate(
        [total[h * rows : (h + 1) * rows] for h in range(width // LANES)], axis=1
    )
    mixed[...] = (hidden[...].astype(F32) + blended).astype(BF16)


def combine(slabs, hidden, select):
    return pl.pallas_call(
        combine_kernel,
        out_shape=jax.ShapeDtypeStruct(hidden.shape, BF16),
        in_specs=in_vmem(3),
        out_specs=in_vmem(1)[0],
        compiler_params=params(),
        name="combine",
    )(slabs, hidden, select)


def exchange_z(slabs):
    return lax.all_to_all(slabs, "attn", 0, 0, axis_index_groups=Z_GROUPS, tiled=True)


def on_device(
    queries,
    stream,
    kv_pool,
    fresh_kv,
    fresh_owner,
    page_table,
    lengths,
    norm_gain,
    router,
    expert_ids,
    w_gate,
    w_up,
    w_down,
):
    n_attn = lax.axis_size("attn")
    pages, kv_local, page_len, page_width = kv_pool.shape
    sect = lax.axis_index("sect")
    where = jnp.stack([sect // 4, sect % 4]).astype(jnp.int32)

    outgoing = pack_pages(fresh_owner[:, 0], fresh_kv.reshape(-1, page_len, page_width), n_attn)
    arrived = lax.all_to_all(outgoing, "attn", 0, 0, tiled=True)
    kv_out, hidden, payload, select = attend(
        page_table,
        lengths,
        queries,
        stream,
        kv_pool.reshape(pages, page_len, page_width),
        arrived,
        norm_gain.reshape(1, -1),
        router,
        expert_ids,
    )

    half_a, half_b = to_rows(exchange_z(payload))
    a = gather4(half_a, along_x)
    b = gather4(half_b, along_y)
    a, b = lax.optimization_barrier((a, b))
    a = gather4(jnp.concatenate(a, axis=0), along_y)
    b = gather4(jnp.concatenate(b, axis=0), along_x)
    other_a = [permute(v, OTHER_CORE) for v in a]
    other_b = [permute(v, OTHER_CORE) for v in b]
    own_a, own_b, for_a, for_b = run_expert(where, a, other_a, b, other_b, w_gate, w_up, w_down)

    sums = add_cores(own_a, own_b, permute(for_a, OTHER_CORE), permute(for_b, OTHER_CORE))
    a = [sums[0]] + [permute(sums[i], along_x(i)) for i in (1, 2, 3)]
    b = [sums[4]] + [permute(sums[4 + i], along_y(i)) for i in (1, 2, 3)]
    sums = add_first(a, b)
    a = [sums[0]] + [permute(sums[i], along_y(i)) for i in (1, 2, 3)]
    b = [sums[4]] + [permute(sums[4 + i], along_x(i)) for i in (1, 2, 3)]
    mixed = combine(exchange_z(to_slabs(a, b)), hidden, select)
    return (mixed, kv_out.reshape(kv_pool.shape))


def solution(mesh):
    return jax.shard_map(
        on_device,
        mesh=mesh,
        in_specs=(
            P("attn", "sect"),
            P("attn", "sect"),
            P("attn", "sect", None, None),
            P("attn", "sect", None, None),
            P("attn", None),
            P("attn", None),
            P("attn", None),
            P("sect"),
            P("sect", None),
            P("attn", None),
            P(None, ("attn", "sect")),
            P(None, ("attn", "sect")),
            P(("attn", "sect"), None),
        ),
        out_specs=(P("attn", "sect"), P("attn", "sect", None, None)),
        check_vma=False,
    )
```

```python
import functools

import jax
import jax.numpy as jnp
from jax import lax
from jax.experimental import pallas as pl
from jax.experimental.pallas import tpu as pltpu
from jax.sharding import PartitionSpec as P

F32 = jnp.float32
BF16 = jnp.bfloat16
EXPERTS = 4
CAPP = 4
OLD_PAGES = 192
CAP = 10
WIDTH = 768
LANES = 128
SLAB = 64
SCALAR_ROW = 30
NZ = 8
ROWS = NZ * CAP
PIECES = 3
AXES = ("attn", "sect")
MIB = 1024 * 1024


def place(z, y, x, c):
    return (z * 4 + (y % 2) * 2 + c) * 8 + (y // 2) * 4 + x


def pairs(move):
    return [
        (place(z, y, x, c), place(*move(z, y, x, c)))
        for z in range(NZ)
        for y in range(4)
        for x in range(4)
        for c in range(2)
    ]


def along_x(step):
    return pairs(lambda z, y, x, c: (z, y, x ^ step, c))


def along_y(step):
    return pairs(lambda z, y, x, c: (z, y ^ step, x, c))


OTHER_CORE = pairs(lambda z, y, x, c: (z, y, x, c ^ 1))
Z_GROUPS = [[z * 4 + r for z in range(NZ)] for r in range(4)]


def permute(value, perm):
    return lax.ppermute(value, AXES, perm)


def gather4(value, along):
    return [value] + [permute(value, along(step)) for step in (1, 2, 3)]


def in_vmem(count):
    return [pl.BlockSpec(memory_space=pltpu.VMEM)] * count


def in_hbm(count):
    return [pl.BlockSpec(memory_space=pltpu.HBM)] * count


def in_smem(count):
    return [pl.BlockSpec(memory_space=pltpu.SMEM)] * count


def params(mib):
    return pltpu.CompilerParams(vmem_limit_bytes=mib * MIB)


def iota(shape, dim):
    return lax.broadcasted_iota(jnp.int32, shape, dim)


def slab_offset(chunk):
    return jnp.where(chunk < 3, chunk * CAP, chunk * CAP + 2)


def pack_pages_kernel(owner, fresh, out, used):
    out[...] = jnp.zeros_like(out)

    def clear(o, carry):
        used[o] = 0
        return carry

    lax.fori_loop(0, used.shape[0], clear, 0)

    def put(p, carry):
        o = owner[0, p]
        k = used[o]
        out[o * CAPP + k] = fresh[p]
        used[o] = k + 1
        return carry

    lax.fori_loop(0, fresh.shape[0], put, 0, unroll=4)


def pack_pages(owners, fresh, n_attn):
    return pl.pallas_call(
        pack_pages_kernel,
        out_shape=jax.ShapeDtypeStruct((n_attn * CAPP,) + fresh.shape[1:], fresh.dtype),
        in_specs=in_smem(1) + in_vmem(1),
        out_specs=in_vmem(1)[0],
        scratch_shapes=[pltpu.SMEM((n_attn,), jnp.int32)],
        compiler_params=params(56),
        name="pack_pages",
    )(owners, fresh)


def split3(value):
    pieces = []
    for _ in range(PIECES):
        piece = value.astype(BF16).astype(F32)
        pieces.append(piece)
        value = value - piece
    return pieces


def find_places(ids, queries, select_out, places_out, heads_out):
    rows, width = queries.shape
    heads = width // LANES
    for h in range(heads):
        heads_out[pl.ds(h, rows, stride=8), :] = queries[:, h * LANES : (h + 1) * LANES].astype(F32)
    for h in range(heads, 8):
        heads_out[pl.ds(h, rows, stride=8), :] = jnp.zeros((rows, LANES), F32)
    ids_f = ids[...].astype(F32)
    cols = EXPERTS * 32
    spread = (iota((rows, cols), 1) % rows == iota((rows, cols), 0)).astype(F32)
    ids_l = jnp.dot(ids_f, spread, preferred_element_type=F32).astype(jnp.int32)
    e0, e1 = ids_l[0:1], ids_l[1:2]
    expert = iota((8, cols), 0)
    routed = ((expert == e0) | (expert == e1)).astype(F32)
    before = ((iota((cols, cols), 0) < rows) & (iota((cols, cols), 0) < iota((cols, cols), 1) % rows)).astype(F32)
    slot = jnp.dot(routed, before, preferred_element_type=F32).astype(jnp.int32)
    slot0 = jnp.sum(jnp.where(expert == e0, slot, 0), axis=0, keepdims=True)
    slot1 = jnp.sum(jnp.where(expert == e1, slot, 0), axis=0, keepdims=True)
    column = iota((1, cols), 1)
    offset = slab_offset(column // rows)
    features = column < heads * rows
    target0 = jnp.where(
        features,
        e0 * SLAB + slot0 + offset,
        jnp.where(column < (heads + 1) * rows, e0 * SLAB + SCALAR_ROW, -1),
    )
    target1 = jnp.where(
        features,
        e1 * SLAB + slot1 + offset,
        jnp.where(column < (heads + 1) * rows, -1, e1 * SLAB + SCALAR_ROW),
    )
    at = iota((EXPERTS * SLAB, cols), 0)
    select_out[...] = ((at == target0) | (at == target1)).astype(F32).astype(BF16)

    diagonal = (iota((rows, cols), 1) == iota((rows, cols), 0)).astype(F32)
    for i, value in enumerate((e0, e1, slot0, slot1)):
        column_of = jnp.sum(diagonal * value.astype(F32), axis=1, keepdims=True)
        places_out[i * rows : (i + 1) * rows, :] = jnp.broadcast_to(
            column_of.astype(jnp.int32), (rows, LANES)
        )


def attend_kernel(
    table,
    lengths,
    *refs,
):
    in_hbm_refs = refs[:8]
    kv_out, hidden_out, payload = refs[8:11]
    pool, heads_v, stream, gain, router, select, places, scores_v, o_scr, sems = refs[11:]
    kv_pool, arrived = in_hbm_refs[:2]
    rows, width = stream.shape
    heads = width // LANES
    pages = table.shape[1]
    fresh = pl.ds(OLD_PAGES, arrived.shape[0])
    kept = pl.ds(0, OLD_PAGES)
    loads = [
        pltpu.make_async_copy(source, target, sems.at[i])
        for i, (source, target) in enumerate(
            [
                (kv_pool.at[kept], pool.at[kept]),
                (arrived, pool.at[fresh]),
                (in_hbm_refs[2], heads_v),
                (in_hbm_refs[3], stream),
                (in_hbm_refs[4], gain),
                (in_hbm_refs[5], router),
                (in_hbm_refs[6], select),
                (in_hbm_refs[7], places),
            ]
        )
    ]
    for load in loads:
        load.start()
    for load in loads[:3]:
        load.wait()
    store = pltpu.make_async_copy(pool, kv_out, sems.at[8])
    store.start()
    scale = float(LANES) ** (-0.5)
    length = jnp.concatenate(
        [jnp.full((8, 1), lengths[0, r], jnp.int32) for r in range(rows)], axis=0
    )
    for r in range(rows):
        keys = jnp.concatenate([pool[table[r, p], :, :LANES] for p in range(pages)], axis=0)
        query = heads_v[r * 8 : (r + 1) * 8, :]
        query = jnp.concatenate([query, query], axis=0).astype(BF16)
        scores = lax.dot_general(query, keys, (((1,), (1,)), ((), ())), preferred_element_type=F32)
        scores_v[r * 8 : (r + 1) * 8, :] = scores[:8]
    scores = scores_v[...] * scale
    valid = iota(scores.shape, 1) < length
    masked = jnp.where(valid, scores, -1e30)
    top = jnp.max(masked, axis=1, keepdims=True)
    weights = jnp.where(valid, jnp.exp(masked - top), 0.0)
    total = jnp.sum(weights, axis=1, keepdims=True)
    scores_v[...] = weights
    for r in range(rows):
        values = jnp.concatenate([pool[table[r, p], :, LANES:] for p in range(pages)], axis=0)
        weight = scores_v[r * 8 : (r + 1) * 8, :]
        weight = jnp.concatenate([weight, weight], axis=0).astype(BF16)
        o_scr[r * 8 : (r + 1) * 8, :] = jnp.dot(weight, values, preferred_element_type=F32)[:8]
    o_scr[...] = o_scr[...] / total
    for load in loads[3:]:
        load.wait()
    attended = jnp.concatenate([o_scr[pl.ds(h, rows, stride=8), :] for h in range(heads)], axis=1)
    hidden = (stream[...].astype(F32) + attended).astype(BF16)
    hidden_out[...] = hidden
    hidden_f = hidden.astype(F32)
    squares = jnp.sum(hidden_f * hidden_f, axis=1, keepdims=True)
    gained = (hidden_f * gain[...].astype(F32)).astype(BF16)
    logits = lax.dot_general(gained, router[...], (((1,), (1,)), ((), ())), preferred_element_type=F32)
    expert_r = iota(logits.shape, 1)
    c0, c1, slot_c0, slot_c1 = [places[i * rows : (i + 1) * rows, :] for i in range(4)]
    delta = jnp.sum(
        jnp.where(expert_r == c0[:, :EXPERTS], logits, 0.0)
        - jnp.where(expert_r == c1[:, :EXPERTS], logits, 0.0),
        axis=1,
        keepdims=True,
    )
    lane = iota((rows, LANES), 1)

    def scalars(slots, difference):
        total = jnp.zeros((rows, LANES), F32)
        for i, piece in enumerate(split3(squares) + split3(difference)):
            total = total + jnp.where(lane == i * CAP + slots, piece, 0.0)
        return total.astype(BF16)

    parts = [gained[:, h * LANES : (h + 1) * LANES] for h in range(heads)]
    parts += [scalars(slot_c0, delta), scalars(slot_c1, -delta)]
    stacked = jnp.concatenate(parts, axis=0)
    slabs = jnp.dot(select[...], stacked, preferred_element_type=F32).astype(BF16)
    for e in range(EXPERTS):
        slab = slabs[e * SLAB : (e + 1) * SLAB]
        payload[2 * e] = slab
        payload[2 * e + 1] = slab
    store.wait()


def attend(table, lengths, kv_pool, arrived, heads, stream, gain, router, select, places):
    rows, width = stream.shape
    shape = jax.ShapeDtypeStruct
    return pl.pallas_call(
        attend_kernel,
        out_shape=(
            shape(kv_pool.shape, kv_pool.dtype),
            shape((rows, width), BF16),
            shape((NZ, SLAB, LANES), BF16),
        ),
        in_specs=in_smem(2) + in_hbm(1) + in_vmem(1) + in_hbm(6),
        out_specs=tuple(in_hbm(1) + in_vmem(2)),
        scratch_shapes=[
            pltpu.VMEM(kv_pool.shape, kv_pool.dtype),
            pltpu.VMEM(heads.shape, F32),
            pltpu.VMEM(stream.shape, BF16),
            pltpu.VMEM(gain.shape, BF16),
            pltpu.VMEM(router.shape, BF16),
            pltpu.VMEM(select.shape, BF16),
            pltpu.VMEM(places.shape, jnp.int32),
            pltpu.VMEM((rows * 8, table.shape[1] * kv_pool.shape[1]), F32),
            pltpu.VMEM((rows * 8, LANES), F32),
            pltpu.SemaphoreType.DMA((9,)),
        ],
        compiler_params=params(56),
        name="attend",
    )(table, lengths, kv_pool, arrived, heads, stream, gain, router, select, places)


def prepare_kernel(where, w_gate, w_up, w_down, ids, queries, *refs):
    made, places, blocks, sems = refs[:6], refs[6:9], refs[9:15], refs[15]
    pieces = []
    for n in range(4):
        x = jnp.bitwise_xor(where[1], n)
        for h in range(2):
            at = pl.ds(pl.multiple_of((h * 4 + x) * WIDTH, WIDTH), WIDTH)
            to = pl.ds(h * WIDTH, WIDTH)
            pieces.append((n, w_gate.at[at, :], blocks[n].at[to, pl.ds(0, LANES)]))
            pieces.append((n, w_up.at[at, :], blocks[n].at[to, pl.ds(LANES, LANES)]))
    for hm in range(2):
        h = jnp.bitwise_xor(where[0], hm)
        for pair in range(12):
            start = pl.multiple_of(h * 4 * WIDTH + pair * 2 * LANES, 2 * LANES)
            to = pl.ds(pair * LANES, LANES)
            pieces.append((4 + hm, w_down.at[:, pl.ds(start, 2 * LANES)], blocks[4 + hm].at[to, :]))
    loads = [
        (n, pltpu.make_async_copy(source, target, sems.at[i]))
        for i, (n, source, target) in enumerate(pieces)
    ]
    for _, load in loads:
        load.start()
    stores = []
    for n in range(6):
        for block, load in loads:
            if block == n:
                load.wait()
        stores.append(pltpu.make_async_copy(blocks[n], made[n], sems.at[40 + n]))
        stores[n].start()
    find_places(ids, queries, *places)
    for store in stores:
        store.wait()


def prepare(where, w_gate, w_up, w_down, ids, queries):
    rows = queries.shape[0]
    block = (2 * WIDTH, 2 * LANES)
    shape = jax.ShapeDtypeStruct
    return pl.pallas_call(
        prepare_kernel,
        out_shape=(shape(block, BF16),) * 6
        + (
            shape((EXPERTS * SLAB, LANES), BF16),
            shape((4 * rows, LANES), jnp.int32),
            shape((rows * 8, LANES), F32),
        ),
        in_specs=in_smem(1) + in_hbm(3) + in_vmem(2),
        out_specs=tuple(in_hbm(6) + in_vmem(3)),
        scratch_shapes=[pltpu.VMEM(block, BF16)] * 6 + [pltpu.SemaphoreType.DMA((46,))],
        compiler_params=params(56),
        name="prepare",
    )(where, w_gate, w_up, w_down, ids, queries)


def to_rows_kernel(slabs, out):
    count = NZ * SLAB
    to, at = iota((count, count), 0), iota((count, count), 1)
    row = to // NZ
    row = jnp.where(row < 3 * CAP, row, row + 2)
    row = jnp.where(row >= SLAB - 2, SCALAR_ROW, row)
    select = ((to % NZ) * SLAB + row == at).astype(F32).astype(BF16)
    flat = slabs[...].reshape(count, LANES)
    out[...] = jnp.dot(select, flat, preferred_element_type=F32).astype(BF16)[: out.shape[0]]


def to_rows(slabs):
    return pl.pallas_call(
        to_rows_kernel,
        out_shape=jax.ShapeDtypeStruct((6 * ROWS + 16, LANES), BF16),
        in_specs=in_vmem(1),
        out_specs=in_vmem(1)[0],
        compiler_params=params(16),
        name="to_rows",
    )(slabs)


BLOCKS = [(c, g) for c in range(2) for g in range(2)]
PART_ROWS = 4 * ROWS + 4 * NZ


def gate_up_kernel(where, *refs):
    rows = (refs[0:4], refs[4:8])
    weights = refs[8:12]
    outs = refs[14:18]
    left = []
    for hm in range(2):
        for chunk in range(6):
            at = slice(chunk * ROWS, (chunk + 1) * ROWS)
            left.append(jnp.concatenate([rows[c][2 * hm + g][at, :] for c, g in BLOCKS], axis=0))
    left = [jnp.concatenate(left[6 * hm : 6 * hm + 6], axis=1) for hm in range(2)]
    scalars = []
    for hm in range(2):
        at = slice(6 * ROWS, 6 * ROWS + 16)
        scalars.append(
            jnp.concatenate([rows[c][2 * hm + g][at, :].astype(F32)[:NZ] for c, g in BLOCKS], axis=0)
        )
    scalars = jnp.concatenate(scalars, axis=1)
    for n in range(4):
        parts = []
        for hm in range(2):
            h = jnp.bitwise_xor(where[0], hm)
            at = pl.ds(pl.multiple_of(h * WIDTH, WIDTH), WIDTH)
            parts.append(jnp.dot(left[hm], weights[n][at, :], preferred_element_type=F32))
        total = parts[0] + parts[1]
        outs[n][: 4 * ROWS, :] = total.astype(outs[n].dtype)
        outs[n][4 * ROWS :, :] = scalars.astype(outs[n].dtype)


def gate_up(where, own, other, weights, later):
    out = jax.ShapeDtypeStruct((PART_ROWS, 2 * LANES), BF16)
    return pl.pallas_call(
        gate_up_kernel,
        out_shape=(jax.ShapeDtypeStruct(out.shape, F32), out, out, out),
        in_specs=in_smem(1) + in_vmem(12) + in_hbm(2),
        out_specs=tuple(in_vmem(4)),
        compiler_params=params(24),
        name="gate_up",
    )(where, *own, *other, *weights, *later)


def activate_kernel(*refs):
    outs = refs[4:6]
    for i, (c, g) in enumerate(BLOCKS):
        sums = jnp.zeros((NZ, 2 * LANES), F32)
        for ref in refs[:4]:
            sums = sums + ref[4 * ROWS :, :].astype(F32)[i * NZ : (i + 1) * NZ]
        sums = sums[:, :LANES] + sums[:, LANES:]

        def scalar(first):
            return sum(
                sums[:, (first + p) * CAP : (first + p + 1) * CAP] for p in range(PIECES)
            )

        inverse = lax.rsqrt(scalar(0) / (WIDTH * 8) + 1e-05)
        gate = 1.0 / (1.0 + jnp.exp(-scalar(PIECES) * inverse))
        at = slice(i * ROWS, (i + 1) * ROWS)
        part = (refs[0][at, :] + refs[1][at, :].astype(F32)) + (
            refs[2][at, :].astype(F32) + refs[3][at, :].astype(F32)
        )
        active = []
        for k in range(CAP):
            rows = part[k * NZ : (k + 1) * NZ] * inverse[:, k : k + 1]
            v, up = rows[:, :LANES], rows[:, LANES:]
            active.append(v / (1.0 + jnp.exp(-v)) * up * gate[:, k : k + 1])
        outs[g][c * ROWS : (c + 1) * ROWS, :] = jnp.concatenate(active, axis=0).astype(BF16)


def activate(parts):
    out = jax.ShapeDtypeStruct((2 * ROWS, LANES), BF16)
    return pl.pallas_call(
        activate_kernel,
        out_shape=(out, out),
        in_specs=in_vmem(4),
        out_specs=tuple(in_vmem(2)),
        compiler_params=params(8),
        name="activate",
    )(*parts)


def down_kernel(where, *refs):
    active, weights, outs = refs[0:4], refs[4:8], refs[8:10]
    left = jnp.concatenate([ref[...] for ref in active], axis=1)
    for n in range(4):
        x = jnp.bitwise_xor(where[1], n)
        for pair in range(3):
            at = pl.ds(pl.multiple_of((x * 3 + pair) * LANES, LANES), LANES)
            right = jnp.concatenate([ref[at, :] for ref in weights], axis=0)
            made = jnp.dot(left, right, preferred_element_type=F32).astype(BF16)
            for c in range(2):
                for half in range(2):
                    chunk = 2 * pair + half
                    outs[c][n, chunk * ROWS : (chunk + 1) * ROWS, :] = made[
                        c * ROWS : (c + 1) * ROWS, half * LANES : (half + 1) * LANES
                    ]


def down(where, active, weights):
    out = jax.ShapeDtypeStruct((4, 6 * ROWS, LANES), BF16)
    return pl.pallas_call(
        down_kernel,
        out_shape=(out, out),
        in_specs=in_smem(1) + in_vmem(8),
        out_specs=tuple(in_vmem(2)),
        compiler_params=params(16),
        name="down",
    )(where, *active, *weights)


def add_cores_kernel(own, other, *outs):
    for m in range(4):
        outs[m][...] = (own[m].astype(F32) + other[m].astype(F32)).astype(BF16)


def add_cores(own, other):
    out = jax.ShapeDtypeStruct(own.shape[1:], BF16)
    return pl.pallas_call(
        add_cores_kernel,
        out_shape=(out,) * 4,
        in_specs=in_vmem(2),
        out_specs=tuple(in_vmem(4)),
        compiler_params=params(8),
        name="add_cores",
    )(own, other)


def to_slabs_kernel(*refs):
    count = NZ * SLAB
    summed = (refs[0][...].astype(F32) + refs[1][...].astype(F32)) + (
        refs[2][...].astype(F32) + refs[3][...].astype(F32)
    )
    to, at = iota((count, 6 * ROWS), 0), iota((count, 6 * ROWS), 1)
    row = jnp.where(at < 3 * ROWS, at // NZ, at // NZ + 2)
    select = ((at % NZ) * SLAB + row == to).astype(F32).astype(BF16)
    moved = jnp.dot(select, summed.astype(BF16), preferred_element_type=F32).astype(BF16)
    refs[4][...] = moved.reshape(NZ, SLAB, LANES)


def to_slabs(parts):
    return pl.pallas_call(
        to_slabs_kernel,
        out_shape=jax.ShapeDtypeStruct((NZ, SLAB, LANES), BF16),
        in_specs=in_vmem(4),
        out_specs=in_vmem(1)[0],
        compiler_params=params(8),
        name="to_slabs",
    )(*parts)


def combine_kernel(slabs, hidden, select, mixed):
    rows, width = hidden.shape
    total = jnp.zeros((LANES, LANES), F32)
    for half in range(2):
        flat = jnp.concatenate([slabs[2 * e + half] for e in range(EXPERTS)], axis=0)
        total = total + lax.dot_general(
            select[...], flat, (((0,), (0,)), ((), ())), preferred_element_type=F32
        )
    blended = jnp.concatenate(
        [total[h * rows : (h + 1) * rows] for h in range(width // LANES)], axis=1
    )
    mixed[...] = (hidden[...].astype(F32) + blended).astype(BF16)


def combine(slabs, hidden, select):
    return pl.pallas_call(
        combine_kernel,
        out_shape=jax.ShapeDtypeStruct(hidden.shape, BF16),
        in_specs=in_vmem(3),
        out_specs=in_vmem(1)[0],
        compiler_params=params(16),
        name="combine",
    )(slabs, hidden, select)


def exchange_z(slabs):
    return lax.all_to_all(slabs, "attn", 0, 0, axis_index_groups=Z_GROUPS, tiled=True)


def on_device(
    queries,
    stream,
    kv_pool,
    fresh_kv,
    fresh_owner,
    page_table,
    lengths,
    norm_gain,
    router,
    expert_ids,
    w_gate,
    w_up,
    w_down,
):
    n_attn = lax.axis_size("attn")
    pages, kv_local, page_len, page_width = kv_pool.shape
    sect = lax.axis_index("sect")
    where = jnp.stack([sect // 4, sect % 4]).astype(jnp.int32)

    *blocks, select, places, heads = prepare(
        where, w_gate, w_up, w_down, expert_ids.T, queries
    )
    first = [blocks[0]] + [permute(blocks[n], along_x(n)) for n in (1, 2, 3)]
    second = [permute(blocks[5], along_y(m)) for m in (2, 3)]
    outgoing = pack_pages(fresh_owner.T, fresh_kv.reshape(-1, page_len, page_width), n_attn)
    arrived = lax.all_to_all(outgoing, "attn", 0, 0, tiled=True)
    kv_out, hidden, payload = attend(
        page_table,
        lengths,
        kv_pool.reshape(pages, page_len, page_width),
        arrived,
        heads,
        stream,
        norm_gain.reshape(1, -1),
        router.T,
        select,
        places,
    )

    near, payload = lax.optimization_barrier((blocks[4], payload))
    second = [blocks[4], permute(near, along_y(1))] + second

    own = gather4(to_rows(exchange_z(payload)), along_y)
    other = [permute(v, OTHER_CORE) for v in own]
    parts = gate_up(where, own, other, first, second[2:])
    active = activate([parts[0]] + [permute(parts[n], along_x(n)) for n in (1, 2, 3)])
    active = [active[0]] + [permute(active[m % 2], along_y(m)) for m in (1, 2, 3)]
    made, for_other = down(where, active, second)
    sums = add_cores(made, permute(for_other, OTHER_CORE))
    slabs = to_slabs([sums[0]] + [permute(sums[n], along_x(n)) for n in (1, 2, 3)])
    mixed = combine(exchange_z(slabs), hidden, select)
    return (mixed, kv_out.reshape(kv_pool.shape))


def solution(mesh):
    return jax.shard_map(
        on_device,
        mesh=mesh,
        in_specs=(
            P("attn", "sect"),
            P("attn", "sect"),
            P("attn", "sect", None, None),
            P("attn", "sect", None, None),
            P("attn", None),
            P("attn", None),
            P("attn", None),
            P("sect"),
            P("sect", None),
            P("attn", None),
            P(None, ("attn", "sect")),
            P(None, ("attn", "sect")),
            P(("attn", "sect"), None),
        ),
        out_specs=(P("attn", "sect"), P("attn", "sect", None, None)),
        check_vma=False,
    )
```

```python
import functools

import jax
import jax.numpy as jnp
from jax import lax
from jax.experimental import pallas as pl
from jax.experimental.pallas import tpu as pltpu
from jax.sharding import PartitionSpec as P

F32 = jnp.float32
BF16 = jnp.bfloat16
EXPERTS = 4
CAPP = 4
OLD_PAGES = 192
CAP = 10
WIDTH = 768
LANES = 128
SLAB = 64
SCALAR_ROW = 30
NZ = 8
ROWS = NZ * CAP
PIECES = 3
AXES = ("attn", "sect")
MIB = 1024 * 1024


def place(z, y, x, c):
    return (z * 4 + (y % 2) * 2 + c) * 8 + (y // 2) * 4 + x


def pairs(move):
    return [
        (place(z, y, x, c), place(*move(z, y, x, c)))
        for z in range(NZ)
        for y in range(4)
        for x in range(4)
        for c in range(2)
    ]


def along_x(step):
    return pairs(lambda z, y, x, c: (z, y, (x + step) % 4, c))


def along_y(step):
    return pairs(lambda z, y, x, c: (z, y ^ step, x, c))


OTHER_CORE = pairs(lambda z, y, x, c: (z, y, x, c ^ 1))
Z_GROUPS = [[z * 4 + r for z in reversed(range(NZ))] for r in range(4)]
PAGE_GROUPS = [[z * 4 + r for z in reversed(range(NZ)) for r in range(4)]]
OWNERS_Z = 4


def permute(value, perm):
    return lax.ppermute(value, AXES, perm)


def gather4(value, along):
    return [value] + [permute(value, along(step)) for step in (1, 2, 3)]


def in_vmem(count):
    return [pl.BlockSpec(memory_space=pltpu.VMEM)] * count


def in_hbm(count):
    return [pl.BlockSpec(memory_space=pltpu.HBM)] * count


def in_smem(count):
    return [pl.BlockSpec(memory_space=pltpu.SMEM)] * count


def params(mib):
    return pltpu.CompilerParams(vmem_limit_bytes=mib * MIB)


def iota(shape, dim):
    return lax.broadcasted_iota(jnp.int32, shape, dim)


def slab_offset(chunk):
    return jnp.where(chunk < 3, chunk * CAP, chunk * CAP + 2)


def pack_pages_kernel(owner, fresh, out, used):
    out[...] = jnp.zeros_like(out)

    def clear(o, carry):
        used[o] = 0
        return carry

    lax.fori_loop(0, used.shape[0], clear, 0)

    def put(p, carry):
        o = owner[0, p]
        k = used[o]
        at = (NZ - 1 - o // OWNERS_Z) * OWNERS_Z + o % OWNERS_Z
        out[at * CAPP + k] = fresh[p]
        used[o] = k + 1
        return carry

    lax.fori_loop(0, fresh.shape[0], put, 0, unroll=4)


def pack_pages(owners, fresh, n_attn):
    return pl.pallas_call(
        pack_pages_kernel,
        out_shape=jax.ShapeDtypeStruct((n_attn * CAPP,) + fresh.shape[1:], fresh.dtype),
        in_specs=in_smem(1) + in_vmem(1),
        out_specs=in_vmem(1)[0],
        scratch_shapes=[pltpu.SMEM((n_attn,), jnp.int32)],
        compiler_params=params(56),
        name="pack_pages",
    )(owners, fresh)


def split3(value):
    pieces = []
    for _ in range(PIECES):
        piece = value.astype(BF16).astype(F32)
        pieces.append(piece)
        value = value - piece
    return pieces


def find_places(ids, queries, select_out, places_out, heads_out):
    rows, width = queries.shape
    heads = width // LANES
    for h in range(heads):
        heads_out[pl.ds(h, rows, stride=8), :] = queries[:, h * LANES : (h + 1) * LANES].astype(F32)
    for h in range(heads, 8):
        heads_out[pl.ds(h, rows, stride=8), :] = jnp.zeros((rows, LANES), F32)
    ids_f = ids[...].astype(F32)
    cols = EXPERTS * 32
    spread = (iota((rows, cols), 1) % rows == iota((rows, cols), 0)).astype(F32)
    ids_l = jnp.dot(ids_f, spread, preferred_element_type=F32).astype(jnp.int32)
    e0, e1 = ids_l[0:1], ids_l[1:2]
    expert = iota((8, cols), 0)
    routed = ((expert == e0) | (expert == e1)).astype(F32)
    before = ((iota((cols, cols), 0) < rows) & (iota((cols, cols), 0) < iota((cols, cols), 1) % rows)).astype(F32)
    slot = jnp.dot(routed, before, preferred_element_type=F32).astype(jnp.int32)
    slot0 = jnp.sum(jnp.where(expert == e0, slot, 0), axis=0, keepdims=True)
    slot1 = jnp.sum(jnp.where(expert == e1, slot, 0), axis=0, keepdims=True)
    column = iota((1, cols), 1)
    offset = slab_offset(column // rows)
    features = column < heads * rows
    target0 = jnp.where(
        features,
        e0 * SLAB + slot0 + offset,
        jnp.where(column < (heads + 1) * rows, e0 * SLAB + SCALAR_ROW, -1),
    )
    target1 = jnp.where(
        features,
        e1 * SLAB + slot1 + offset,
        jnp.where(column < (heads + 1) * rows, -1, e1 * SLAB + SCALAR_ROW),
    )
    at = iota((EXPERTS * SLAB, cols), 0)
    select_out[...] = ((at == target0) | (at == target1)).astype(F32).astype(BF16)

    diagonal = (iota((rows, cols), 1) == iota((rows, cols), 0)).astype(F32)
    for i, value in enumerate((e0, e1, slot0, slot1)):
        column_of = jnp.sum(diagonal * value.astype(F32), axis=1, keepdims=True)
        places_out[i * rows : (i + 1) * rows, :] = jnp.broadcast_to(
            column_of.astype(jnp.int32), (rows, LANES)
        )


def attend_kernel(
    table,
    lengths,
    *refs,
):
    in_hbm_refs = refs[:8]
    kv_out, hidden_out, payload = refs[8:11]
    pool, heads_v, stream, gain, router, select, places, scores_v, o_scr, sems = refs[11:]
    kv_pool, arrived = in_hbm_refs[:2]
    rows, width = stream.shape
    heads = width // LANES
    pages = table.shape[1]
    kept = pl.ds(0, OLD_PAGES)
    share = arrived.shape[0] // NZ
    loads = [
        pltpu.make_async_copy(source, target, sems.at[i])
        for i, (source, target) in enumerate(
            [
                (kv_pool.at[kept], pool.at[kept]),
                (in_hbm_refs[2], heads_v),
                (in_hbm_refs[3], stream),
                (in_hbm_refs[4], gain),
                (in_hbm_refs[5], router),
                (in_hbm_refs[6], select),
                (in_hbm_refs[7], places),
            ]
        )
    ]
    for load in loads:
        load.start()
    for z in range(NZ):
        to, at = OLD_PAGES + z * share, (NZ - 1 - z) * share
        pool[to : to + share] = arrived[at : at + share]
    for load in loads[:2]:
        load.wait()
    store = pltpu.make_async_copy(pool, kv_out, sems.at[7])
    store.start()
    scale = float(LANES) ** (-0.5)
    length = jnp.concatenate(
        [jnp.full((8, 1), lengths[0, r], jnp.int32) for r in range(rows)], axis=0
    )
    for r in range(rows):
        keys = jnp.concatenate([pool[table[r, p], :, :LANES] for p in range(pages)], axis=0)
        query = heads_v[r * 8 : (r + 1) * 8, :]
        query = jnp.concatenate([query, query], axis=0).astype(BF16)
        scores = lax.dot_general(query, keys, (((1,), (1,)), ((), ())), preferred_element_type=F32)
        scores_v[r * 8 : (r + 1) * 8, :] = scores[:8]
    scores = scores_v[...] * scale
    valid = iota(scores.shape, 1) < length
    masked = jnp.where(valid, scores, -1e30)
    top = jnp.max(masked, axis=1, keepdims=True)
    weights = jnp.where(valid, jnp.exp(masked - top), 0.0)
    total = jnp.sum(weights, axis=1, keepdims=True)
    scores_v[...] = weights
    for r in range(rows):
        values = jnp.concatenate([pool[table[r, p], :, LANES:] for p in range(pages)], axis=0)
        weight = scores_v[r * 8 : (r + 1) * 8, :]
        weight = jnp.concatenate([weight, weight], axis=0).astype(BF16)
        o_scr[r * 8 : (r + 1) * 8, :] = jnp.dot(weight, values, preferred_element_type=F32)[:8]
    o_scr[...] = o_scr[...] / total
    for load in loads[2:]:
        load.wait()
    attended = jnp.concatenate([o_scr[pl.ds(h, rows, stride=8), :] for h in range(heads)], axis=1)
    hidden = (stream[...].astype(F32) + attended).astype(BF16)
    hidden_out[...] = hidden
    hidden_f = hidden.astype(F32)
    squares = jnp.sum(hidden_f * hidden_f, axis=1, keepdims=True)
    gained = (hidden_f * gain[...].astype(F32)).astype(BF16)
    logits = lax.dot_general(gained, router[...], (((1,), (1,)), ((), ())), preferred_element_type=F32)
    expert_r = iota(logits.shape, 1)
    c0, c1, slot_c0, slot_c1 = [places[i * rows : (i + 1) * rows, :] for i in range(4)]
    delta = jnp.sum(
        jnp.where(expert_r == c0[:, :EXPERTS], logits, 0.0)
        - jnp.where(expert_r == c1[:, :EXPERTS], logits, 0.0),
        axis=1,
        keepdims=True,
    )
    lane = iota((rows, LANES), 1)

    def scalars(slots, difference):
        total = jnp.zeros((rows, LANES), F32)
        for i, piece in enumerate(split3(squares) + split3(difference)):
            total = total + jnp.where(lane == i * CAP + slots, piece, 0.0)
        return total.astype(BF16)

    parts = [gained[:, h * LANES : (h + 1) * LANES] for h in range(heads)]
    parts += [scalars(slot_c0, delta), scalars(slot_c1, -delta)]
    stacked = jnp.concatenate(parts, axis=0)
    slabs = jnp.dot(select[...], stacked, preferred_element_type=F32).astype(BF16)
    for e in range(EXPERTS):
        slab = slabs[e * SLAB : (e + 1) * SLAB]
        payload[NZ - 1 - 2 * e] = slab
        payload[NZ - 2 - 2 * e] = slab
    store.wait()


def attend(table, lengths, kv_pool, arrived, heads, stream, gain, router, select, places):
    rows, width = stream.shape
    shape = jax.ShapeDtypeStruct
    return pl.pallas_call(
        attend_kernel,
        out_shape=(
            shape(kv_pool.shape, kv_pool.dtype),
            shape((rows, width), BF16),
            shape((NZ, SLAB, LANES), BF16),
        ),
        in_specs=in_smem(2) + in_hbm(1) + in_vmem(1) + in_hbm(6),
        out_specs=tuple(in_hbm(1) + in_vmem(2)),
        scratch_shapes=[
            pltpu.VMEM(kv_pool.shape, kv_pool.dtype),
            pltpu.VMEM(heads.shape, F32),
            pltpu.VMEM(stream.shape, BF16),
            pltpu.VMEM(gain.shape, BF16),
            pltpu.VMEM(router.shape, BF16),
            pltpu.VMEM(select.shape, BF16),
            pltpu.VMEM(places.shape, jnp.int32),
            pltpu.VMEM((rows * 8, table.shape[1] * kv_pool.shape[1]), F32),
            pltpu.VMEM((rows * 8, LANES), F32),
            pltpu.SemaphoreType.DMA((8,)),
        ],
        compiler_params=params(56),
        name="attend",
    )(table, lengths, kv_pool, arrived, heads, stream, gain, router, select, places)


def prepare_kernel(where, w_gate, w_up, w_down, ids, queries, *refs):
    made, places, blocks, sems = refs[:6], refs[6:9], refs[9:15], refs[15]
    pieces = []
    for n in range(4):
        x = jnp.bitwise_and(where[1] + n, 3)
        for h in range(2):
            at = pl.ds(pl.multiple_of((h * 4 + x) * WIDTH, WIDTH), WIDTH)
            to = pl.ds(h * WIDTH, WIDTH)
            pieces.append((n, w_gate.at[at, :], blocks[n].at[to, pl.ds(0, LANES)]))
            pieces.append((n, w_up.at[at, :], blocks[n].at[to, pl.ds(LANES, LANES)]))
    for hm in range(2):
        h = jnp.bitwise_xor(where[0], hm)
        for pair in range(12):
            start = pl.multiple_of(h * 4 * WIDTH + pair * 2 * LANES, 2 * LANES)
            to = pl.ds(pair * LANES, LANES)
            pieces.append((4 + hm, w_down.at[:, pl.ds(start, 2 * LANES)], blocks[4 + hm].at[to, :]))
    loads = [
        (n, pltpu.make_async_copy(source, target, sems.at[i]))
        for i, (n, source, target) in enumerate(pieces)
    ]
    for _, load in loads:
        load.start()
    stores = []
    for n in range(6):
        for block, load in loads:
            if block == n:
                load.wait()
        stores.append(pltpu.make_async_copy(blocks[n], made[n], sems.at[40 + n]))
        stores[n].start()
    find_places(ids, queries, *places)
    for store in stores:
        store.wait()


def prepare(where, w_gate, w_up, w_down, ids, queries):
    rows = queries.shape[0]
    block = (2 * WIDTH, 2 * LANES)
    shape = jax.ShapeDtypeStruct
    return pl.pallas_call(
        prepare_kernel,
        out_shape=(shape(block, BF16),) * 6
        + (
            shape((EXPERTS * SLAB, LANES), BF16),
            shape((4 * rows, LANES), jnp.int32),
            shape((rows * 8, LANES), F32),
        ),
        in_specs=in_smem(1) + in_hbm(3) + in_vmem(2),
        out_specs=tuple(in_hbm(6) + in_vmem(3)),
        scratch_shapes=[pltpu.VMEM(block, BF16)] * 6 + [pltpu.SemaphoreType.DMA((46,))],
        compiler_params=params(56),
        name="prepare",
    )(where, w_gate, w_up, w_down, ids, queries)


def to_rows_kernel(slabs, out):
    count = NZ * SLAB
    to, at = iota((count, count), 0), iota((count, count), 1)
    row = to // NZ
    row = jnp.where(row < 3 * CAP, row, row + 2)
    row = jnp.where(row >= SLAB - 2, SCALAR_ROW, row)
    select = ((to % NZ) * SLAB + row == at).astype(F32).astype(BF16)
    flat = slabs[...].reshape(count, LANES)
    out[...] = jnp.dot(select, flat, preferred_element_type=F32).astype(BF16)[: out.shape[0]]


def to_rows(slabs):
    return pl.pallas_call(
        to_rows_kernel,
        out_shape=jax.ShapeDtypeStruct((6 * ROWS + 16, LANES), BF16),
        in_specs=in_vmem(1),
        out_specs=in_vmem(1)[0],
        compiler_params=params(16),
        name="to_rows",
    )(slabs)


BLOCKS = [(c, g) for c in range(2) for g in range(2)]
PART_ROWS = 4 * ROWS + 4 * NZ


def gate_up_kernel(where, *refs):
    rows = (refs[0:4], refs[4:8])
    weights = refs[8:12]
    outs = refs[14:18]
    left = []
    for hm in range(2):
        for chunk in range(6):
            at = slice(chunk * ROWS, (chunk + 1) * ROWS)
            left.append(jnp.concatenate([rows[c][2 * hm + g][at, :] for c, g in BLOCKS], axis=0))
    left = [jnp.concatenate(left[6 * hm : 6 * hm + 6], axis=1) for hm in range(2)]
    scalars = []
    for hm in range(2):
        at = slice(6 * ROWS, 6 * ROWS + 16)
        scalars.append(
            jnp.concatenate([rows[c][2 * hm + g][at, :].astype(F32)[:NZ] for c, g in BLOCKS], axis=0)
        )
    scalars = jnp.concatenate(scalars, axis=1)
    for n in range(4):
        parts = []
        for hm in range(2):
            h = jnp.bitwise_xor(where[0], hm)
            at = pl.ds(pl.multiple_of(h * WIDTH, WIDTH), WIDTH)
            parts.append(jnp.dot(left[hm], weights[n][at, :], preferred_element_type=F32))
        total = parts[0] + parts[1]
        outs[n][: 4 * ROWS, :] = total.astype(outs[n].dtype)
        outs[n][4 * ROWS :, :] = scalars.astype(outs[n].dtype)


def gate_up(where, own, other, weights, later):
    out = jax.ShapeDtypeStruct((PART_ROWS, 2 * LANES), BF16)
    return pl.pallas_call(
        gate_up_kernel,
        out_shape=(jax.ShapeDtypeStruct(out.shape, F32), out, out, out),
        in_specs=in_smem(1) + in_vmem(12) + in_hbm(2),
        out_specs=tuple(in_vmem(4)),
        compiler_params=params(24),
        name="gate_up",
    )(where, *own, *other, *weights, *later)


def activate_kernel(*refs):
    outs = refs[4:6]
    for i, (c, g) in enumerate(BLOCKS):
        sums = jnp.zeros((NZ, 2 * LANES), F32)
        for ref in refs[:4]:
            sums = sums + ref[4 * ROWS :, :].astype(F32)[i * NZ : (i + 1) * NZ]
        sums = sums[:, :LANES] + sums[:, LANES:]

        def scalar(first):
            return sum(
                sums[:, (first + p) * CAP : (first + p + 1) * CAP] for p in range(PIECES)
            )

        inverse = lax.rsqrt(scalar(0) / (WIDTH * 8) + 1e-05)
        gate = 1.0 / (1.0 + jnp.exp(-scalar(PIECES) * inverse))
        at = slice(i * ROWS, (i + 1) * ROWS)
        part = (refs[0][at, :] + refs[1][at, :].astype(F32)) + (
            refs[2][at, :].astype(F32) + refs[3][at, :].astype(F32)
        )
        active = []
        for k in range(CAP):
            rows = part[k * NZ : (k + 1) * NZ] * inverse[:, k : k + 1]
            v, up = rows[:, :LANES], rows[:, LANES:]
            active.append(v / (1.0 + jnp.exp(-v)) * up * gate[:, k : k + 1])
        outs[g][c * ROWS : (c + 1) * ROWS, :] = jnp.concatenate(active, axis=0).astype(BF16)


def activate(parts):
    out = jax.ShapeDtypeStruct((2 * ROWS, LANES), BF16)
    return pl.pallas_call(
        activate_kernel,
        out_shape=(out, out),
        in_specs=in_vmem(4),
        out_specs=tuple(in_vmem(2)),
        compiler_params=params(8),
        name="activate",
    )(*parts)


def down_kernel(where, *refs):
    active, weights, outs = refs[0:4], refs[4:8], refs[8:10]
    left = jnp.concatenate([ref[...] for ref in active], axis=1)
    for n in range(4):
        x = jnp.bitwise_and(where[1] + n, 3)
        for pair in range(3):
            at = pl.ds(pl.multiple_of((x * 3 + pair) * LANES, LANES), LANES)
            right = jnp.concatenate([ref[at, :] for ref in weights], axis=0)
            made = jnp.dot(left, right, preferred_element_type=F32).astype(BF16)
            for c in range(2):
                for half in range(2):
                    chunk = 2 * pair + half
                    outs[c][n, chunk * ROWS : (chunk + 1) * ROWS, :] = made[
                        c * ROWS : (c + 1) * ROWS, half * LANES : (half + 1) * LANES
                    ]


def down(where, active, weights):
    out = jax.ShapeDtypeStruct((4, 6 * ROWS, LANES), BF16)
    return pl.pallas_call(
        down_kernel,
        out_shape=(out, out),
        in_specs=in_smem(1) + in_vmem(8),
        out_specs=tuple(in_vmem(2)),
        compiler_params=params(16),
        name="down",
    )(where, *active, *weights)


def add_cores_kernel(own, other, *outs):
    for m in range(4):
        outs[m][...] = (own[m].astype(F32) + other[m].astype(F32)).astype(BF16)


def add_cores(own, other):
    out = jax.ShapeDtypeStruct(own.shape[1:], BF16)
    return pl.pallas_call(
        add_cores_kernel,
        out_shape=(out,) * 4,
        in_specs=in_vmem(2),
        out_specs=tuple(in_vmem(4)),
        compiler_params=params(8),
        name="add_cores",
    )(own, other)


def to_slabs_kernel(*refs):
    count = NZ * SLAB
    summed = (refs[0][...].astype(F32) + refs[1][...].astype(F32)) + (
        refs[2][...].astype(F32) + refs[3][...].astype(F32)
    )
    to, at = iota((count, 6 * ROWS), 0), iota((count, 6 * ROWS), 1)
    row = jnp.where(at < 3 * ROWS, at // NZ, at // NZ + 2)
    select = ((at % NZ) * SLAB + row == to).astype(F32).astype(BF16)
    moved = jnp.dot(select, summed.astype(BF16), preferred_element_type=F32).astype(BF16)
    refs[4][...] = moved.reshape(NZ, SLAB, LANES)


def to_slabs(parts):
    return pl.pallas_call(
        to_slabs_kernel,
        out_shape=jax.ShapeDtypeStruct((NZ, SLAB, LANES), BF16),
        in_specs=in_vmem(4),
        out_specs=in_vmem(1)[0],
        compiler_params=params(8),
        name="to_slabs",
    )(*parts)


def combine_kernel(slabs, hidden, select, mixed):
    rows, width = hidden.shape
    total = jnp.zeros((LANES, LANES), F32)
    for half in range(2):
        flat = jnp.concatenate([slabs[NZ - 1 - 2 * e - half] for e in range(EXPERTS)], axis=0)
        total = total + lax.dot_general(
            select[...], flat, (((0,), (0,)), ((), ())), preferred_element_type=F32
        )
    blended = jnp.concatenate(
        [total[h * rows : (h + 1) * rows] for h in range(width // LANES)], axis=1
    )
    mixed[...] = (hidden[...].astype(F32) + blended).astype(BF16)


def combine(slabs, hidden, select):
    return pl.pallas_call(
        combine_kernel,
        out_shape=jax.ShapeDtypeStruct(hidden.shape, BF16),
        in_specs=in_vmem(3),
        out_specs=in_vmem(1)[0],
        compiler_params=params(16),
        name="combine",
    )(slabs, hidden, select)


def exchange_z(slabs):
    return lax.all_to_all(slabs, "attn", 0, 0, axis_index_groups=Z_GROUPS, tiled=True)


def on_device(
    queries,
    stream,
    kv_pool,
    fresh_kv,
    fresh_owner,
    page_table,
    lengths,
    norm_gain,
    router,
    expert_ids,
    w_gate,
    w_up,
    w_down,
):
    n_attn = lax.axis_size("attn")
    pages, kv_local, page_len, page_width = kv_pool.shape
    sect = lax.axis_index("sect")
    where = jnp.stack([sect // 4, sect % 4]).astype(jnp.int32)

    *blocks, select, places, heads = prepare(
        where, w_gate, w_up, w_down, expert_ids.T, queries
    )
    first = [blocks[0]] + [permute(blocks[n], along_x(n)) for n in (1, 2, 3)]
    second = [permute(blocks[5], along_y(m)) for m in (2, 3)]
    outgoing = pack_pages(fresh_owner.T, fresh_kv.reshape(-1, page_len, page_width), n_attn)
    arrived = lax.all_to_all(
        outgoing, "attn", 0, 0, axis_index_groups=PAGE_GROUPS, tiled=True
    )
    kv_out, hidden, payload = attend(
        page_table,
        lengths,
        kv_pool.reshape(pages, page_len, page_width),
        arrived,
        heads,
        stream,
        norm_gain.reshape(1, -1),
        router.T,
        select,
        places,
    )

    own = gather4(to_rows(exchange_z(payload)), along_y)
    other = [permute(v, OTHER_CORE) for v in own]
    parts = gate_up(where, own, other, first, second)
    near, *parts = lax.optimization_barrier((blocks[4], *parts))
    second = [blocks[4], permute(near, along_y(1))] + second
    active = activate([parts[0]] + [permute(parts[n], along_x(-n)) for n in (1, 2, 3)])
    active = [active[0]] + [permute(active[m % 2], along_y(m)) for m in (1, 2, 3)]
    made, for_other = down(where, active, second)
    sums = add_cores(made, permute(for_other, OTHER_CORE))
    slabs = to_slabs([sums[0]] + [permute(sums[n], along_x(n)) for n in (1, 2, 3)])
    mixed = combine(exchange_z(slabs), hidden, select)
    return (mixed, kv_out.reshape(kv_pool.shape))


def solution(mesh):
    return jax.shard_map(
        on_device,
        mesh=mesh,
        in_specs=(
            P("attn", "sect"),
            P("attn", "sect"),
            P("attn", "sect", None, None),
            P("attn", "sect", None, None),
            P("attn", None),
            P("attn", None),
            P("attn", None),
            P("sect"),
            P("sect", None),
            P("attn", None),
            P(None, ("attn", "sect")),
            P(None, ("attn", "sect")),
            P(("attn", "sect"), None),
        ),
        out_specs=(P("attn", "sect"), P("attn", "sect", None, None)),
        check_vma=False,
    )
```

```python
import functools

import jax
import jax.numpy as jnp
from jax import lax
from jax.experimental import pallas as pl
from jax.experimental.pallas import tpu as pltpu
from jax.sharding import PartitionSpec as P

F32 = jnp.float32
BF16 = jnp.bfloat16
EXPERTS = 4
CAPP = 4
OLD_PAGES = 192
CAP = 10
WIDTH = 768
LANES = 128
SLAB = 64
SCALAR_ROW = 30
NZ = 8
ROWS = NZ * CAP
PIECES = 3
AXES = ("attn", "sect")
MIB = 1024 * 1024


def place(z, y, x, c):
    return (z * 4 + (y % 2) * 2 + c) * 8 + (y // 2) * 4 + x


def pairs(move):
    return [
        (place(z, y, x, c), place(*move(z, y, x, c)))
        for z in range(NZ)
        for y in range(4)
        for x in range(4)
        for c in range(2)
    ]


def along_x(step):
    return pairs(lambda z, y, x, c: (z, y, (x + step) % 4, c))


def along_y(step):
    return pairs(lambda z, y, x, c: (z, y ^ step, x, c))


OTHER_CORE = pairs(lambda z, y, x, c: (z, y, x, c ^ 1))
Z_GROUPS = [[z * 4 + r for z in reversed(range(NZ))] for r in range(4)]
PAGE_GROUPS = [[z * 4 + r for z in reversed(range(NZ)) for r in range(4)]]
OWNERS_Z = 4


def permute(value, perm):
    return lax.ppermute(value, AXES, perm)


def gather4(value, along):
    return [value] + [permute(value, along(step)) for step in (1, 2, 3)]


def in_vmem(count):
    return [pl.BlockSpec(memory_space=pltpu.VMEM)] * count


def in_hbm(count):
    return [pl.BlockSpec(memory_space=pltpu.HBM)] * count


def in_smem(count):
    return [pl.BlockSpec(memory_space=pltpu.SMEM)] * count


def params(mib):
    return pltpu.CompilerParams(vmem_limit_bytes=mib * MIB)


def iota(shape, dim):
    return lax.broadcasted_iota(jnp.int32, shape, dim)


def slab_offset(chunk):
    return jnp.where(chunk < 3, chunk * CAP, chunk * CAP + 2)


def pack_pages_kernel(owner, fresh, out, used):
    out[...] = jnp.zeros_like(out)

    def clear(o, carry):
        used[o] = 0
        return carry

    lax.fori_loop(0, used.shape[0], clear, 0)

    def put(p, carry):
        o = owner[0, p]
        k = used[o]
        at = (NZ - 1 - o // OWNERS_Z) * OWNERS_Z + o % OWNERS_Z
        out[at * CAPP + k] = fresh[p]
        used[o] = k + 1
        return carry

    lax.fori_loop(0, fresh.shape[0], put, 0, unroll=4)


def pack_pages(owners, fresh, n_attn):
    return pl.pallas_call(
        pack_pages_kernel,
        out_shape=jax.ShapeDtypeStruct((n_attn * CAPP,) + fresh.shape[1:], fresh.dtype),
        in_specs=in_smem(1) + in_vmem(1),
        out_specs=in_vmem(1)[0],
        scratch_shapes=[pltpu.SMEM((n_attn,), jnp.int32)],
        compiler_params=params(56),
        name="pack_pages",
    )(owners, fresh)


def split3(value):
    pieces = []
    for _ in range(PIECES):
        piece = value.astype(BF16).astype(F32)
        pieces.append(piece)
        value = value - piece
    return pieces


def find_places(ids, queries, select_out, places_out, heads_out):
    rows, width = queries.shape
    heads = width // LANES
    for h in range(heads):
        heads_out[pl.ds(h, rows, stride=8), :] = queries[:, h * LANES : (h + 1) * LANES].astype(F32)
    for h in range(heads, 8):
        heads_out[pl.ds(h, rows, stride=8), :] = jnp.zeros((rows, LANES), F32)
    ids_f = ids[...].astype(F32)
    cols = EXPERTS * 32
    spread = (iota((rows, cols), 1) % rows == iota((rows, cols), 0)).astype(F32)
    ids_l = jnp.dot(ids_f, spread, preferred_element_type=F32).astype(jnp.int32)
    e0, e1 = ids_l[0:1], ids_l[1:2]
    expert = iota((8, cols), 0)
    routed = ((expert == e0) | (expert == e1)).astype(F32)
    before = ((iota((cols, cols), 0) < rows) & (iota((cols, cols), 0) < iota((cols, cols), 1) % rows)).astype(F32)
    slot = jnp.dot(routed, before, preferred_element_type=F32).astype(jnp.int32)
    slot0 = jnp.sum(jnp.where(expert == e0, slot, 0), axis=0, keepdims=True)
    slot1 = jnp.sum(jnp.where(expert == e1, slot, 0), axis=0, keepdims=True)
    column = iota((1, cols), 1)
    offset = slab_offset(column // rows)
    features = column < heads * rows
    target0 = jnp.where(
        features,
        e0 * SLAB + slot0 + offset,
        jnp.where(column < (heads + 1) * rows, e0 * SLAB + SCALAR_ROW, -1),
    )
    target1 = jnp.where(
        features,
        e1 * SLAB + slot1 + offset,
        jnp.where(column < (heads + 1) * rows, -1, e1 * SLAB + SCALAR_ROW),
    )
    at = iota((EXPERTS * SLAB, cols), 0)
    select_out[...] = ((at == target0) | (at == target1)).astype(F32).astype(BF16)

    diagonal = (iota((rows, cols), 1) == iota((rows, cols), 0)).astype(F32)
    for i, value in enumerate((e0, e1, slot0, slot1)):
        column_of = jnp.sum(diagonal * value.astype(F32), axis=1, keepdims=True)
        places_out[i * rows : (i + 1) * rows, :] = jnp.broadcast_to(
            column_of.astype(jnp.int32), (rows, LANES)
        )


def attend_kernel(
    table,
    lengths,
    *refs,
):
    in_hbm_refs = refs[:8]
    kv_out, hidden_out, payload = refs[8:11]
    pool, heads_v, stream, gain, router, select, places, scores_v, o_scr, sems = refs[11:]
    kv_pool, arrived = in_hbm_refs[:2]
    rows, width = stream.shape
    heads = width // LANES
    pages = table.shape[1]
    kept = pl.ds(0, OLD_PAGES)
    share = arrived.shape[0] // NZ
    loads = [
        pltpu.make_async_copy(source, target, sems.at[i])
        for i, (source, target) in enumerate(
            [
                (kv_pool.at[kept], pool.at[kept]),
                (in_hbm_refs[2], heads_v),
                (in_hbm_refs[3], stream),
                (in_hbm_refs[4], gain),
                (in_hbm_refs[5], router),
                (in_hbm_refs[6], select),
                (in_hbm_refs[7], places),
            ]
        )
    ]
    for load in loads:
        load.start()
    for z in range(NZ):
        to, at = OLD_PAGES + z * share, (NZ - 1 - z) * share
        pool[to : to + share] = arrived[at : at + share]
    for load in loads[:2]:
        load.wait()
    store = pltpu.make_async_copy(pool, kv_out, sems.at[7])
    store.start()
    scale = float(LANES) ** (-0.5)
    length = jnp.concatenate(
        [jnp.full((8, 1), lengths[0, r], jnp.int32) for r in range(rows)], axis=0
    )
    for r in range(rows):
        keys = jnp.concatenate([pool[table[r, p], :, :LANES] for p in range(pages)], axis=0)
        query = heads_v[r * 8 : (r + 1) * 8, :]
        query = jnp.concatenate([query, query], axis=0).astype(BF16)
        scores = lax.dot_general(query, keys, (((1,), (1,)), ((), ())), preferred_element_type=F32)
        scores_v[r * 8 : (r + 1) * 8, :] = scores[:8]
    scores = scores_v[...] * scale
    valid = iota(scores.shape, 1) < length
    masked = jnp.where(valid, scores, -1e30)
    top = jnp.max(masked, axis=1, keepdims=True)
    weights = jnp.where(valid, jnp.exp(masked - top), 0.0)
    total = jnp.sum(weights, axis=1, keepdims=True)
    scores_v[...] = weights
    for r in range(rows):
        values = jnp.concatenate([pool[table[r, p], :, LANES:] for p in range(pages)], axis=0)
        weight = scores_v[r * 8 : (r + 1) * 8, :]
        weight = jnp.concatenate([weight, weight], axis=0).astype(BF16)
        o_scr[r * 8 : (r + 1) * 8, :] = jnp.dot(weight, values, preferred_element_type=F32)[:8]
    o_scr[...] = o_scr[...] / total
    for load in loads[2:]:
        load.wait()
    attended = jnp.concatenate([o_scr[pl.ds(h, rows, stride=8), :] for h in range(heads)], axis=1)
    hidden = (stream[...].astype(F32) + attended).astype(BF16)
    hidden_out[...] = hidden
    hidden_f = hidden.astype(F32)
    squares = jnp.sum(hidden_f * hidden_f, axis=1, keepdims=True)
    gained = (hidden_f * gain[...].astype(F32)).astype(BF16)
    logits = lax.dot_general(gained, router[...], (((1,), (1,)), ((), ())), preferred_element_type=F32)
    expert_r = iota(logits.shape, 1)
    c0, c1, slot_c0, slot_c1 = [places[i * rows : (i + 1) * rows, :] for i in range(4)]
    delta = jnp.sum(
        jnp.where(expert_r == c0[:, :EXPERTS], logits, 0.0)
        - jnp.where(expert_r == c1[:, :EXPERTS], logits, 0.0),
        axis=1,
        keepdims=True,
    )
    lane = iota((rows, LANES), 1)

    def scalars(slots, difference):
        total = jnp.zeros((rows, LANES), F32)
        for i, piece in enumerate(split3(squares) + split3(difference)):
            total = total + jnp.where(lane == i * CAP + slots, piece, 0.0)
        return total.astype(BF16)

    parts = [gained[:, h * LANES : (h + 1) * LANES] for h in range(heads)]
    parts += [scalars(slot_c0, delta), scalars(slot_c1, -delta)]
    stacked = jnp.concatenate(parts, axis=0)
    slabs = jnp.dot(select[...], stacked, preferred_element_type=F32).astype(BF16)
    for e in range(EXPERTS):
        slab = slabs[e * SLAB : (e + 1) * SLAB]
        payload[NZ - 1 - 2 * e] = slab
        payload[NZ - 2 - 2 * e] = slab
    store.wait()


def attend(table, lengths, kv_pool, arrived, heads, stream, gain, router, select, places):
    rows, width = stream.shape
    shape = jax.ShapeDtypeStruct
    return pl.pallas_call(
        attend_kernel,
        out_shape=(
            shape(kv_pool.shape, kv_pool.dtype),
            shape((rows, width), BF16),
            shape((NZ, SLAB, LANES), BF16),
        ),
        in_specs=in_smem(2) + in_hbm(1) + in_vmem(1) + in_hbm(6),
        out_specs=tuple(in_hbm(1) + in_vmem(2)),
        scratch_shapes=[
            pltpu.VMEM(kv_pool.shape, kv_pool.dtype),
            pltpu.VMEM(heads.shape, F32),
            pltpu.VMEM(stream.shape, BF16),
            pltpu.VMEM(gain.shape, BF16),
            pltpu.VMEM(router.shape, BF16),
            pltpu.VMEM(select.shape, BF16),
            pltpu.VMEM(places.shape, jnp.int32),
            pltpu.VMEM((rows * 8, table.shape[1] * kv_pool.shape[1]), F32),
            pltpu.VMEM((rows * 8, LANES), F32),
            pltpu.SemaphoreType.DMA((8,)),
        ],
        compiler_params=params(56),
        name="attend",
    )(table, lengths, kv_pool, arrived, heads, stream, gain, router, select, places)


def prepare_kernel(where, w_gate, w_up, w_down, ids, queries, *refs):
    made, places, blocks, sems = refs[:6], refs[6:9], refs[9:15], refs[15]
    pieces = []
    for n in range(4):
        x = jnp.bitwise_and(where[1] + n, 3)
        for h in range(2):
            at = pl.ds(pl.multiple_of((h * 4 + x) * WIDTH, WIDTH), WIDTH)
            to = pl.ds(h * WIDTH, WIDTH)
            pieces.append((n, w_gate.at[at, :], blocks[n].at[to, pl.ds(0, LANES)]))
            pieces.append((n, w_up.at[at, :], blocks[n].at[to, pl.ds(LANES, LANES)]))
    for hm in range(2):
        h = jnp.bitwise_xor(where[0], hm)
        for pair in range(12):
            start = pl.multiple_of(h * 4 * WIDTH + pair * 2 * LANES, 2 * LANES)
            to = pl.ds(pair * LANES, LANES)
            pieces.append((4 + hm, w_down.at[:, pl.ds(start, 2 * LANES)], blocks[4 + hm].at[to, :]))
    loads = [
        (n, pltpu.make_async_copy(source, target, sems.at[i]))
        for i, (n, source, target) in enumerate(pieces)
    ]
    for _, load in loads:
        load.start()
    stores = []
    for n in range(6):
        for block, load in loads:
            if block == n:
                load.wait()
        stores.append(pltpu.make_async_copy(blocks[n], made[n], sems.at[40 + n]))
        stores[n].start()
    find_places(ids, queries, *places)
    for store in stores:
        store.wait()


def prepare(where, w_gate, w_up, w_down, ids, queries):
    rows = queries.shape[0]
    block = (2 * WIDTH, 2 * LANES)
    shape = jax.ShapeDtypeStruct
    return pl.pallas_call(
        prepare_kernel,
        out_shape=(shape(block, BF16),) * 6
        + (
            shape((EXPERTS * SLAB, LANES), BF16),
            shape((4 * rows, LANES), jnp.int32),
            shape((rows * 8, LANES), F32),
        ),
        in_specs=in_smem(1) + in_hbm(3) + in_vmem(2),
        out_specs=tuple(in_hbm(6) + in_vmem(3)),
        scratch_shapes=[pltpu.VMEM(block, BF16)] * 6 + [pltpu.SemaphoreType.DMA((46,))],
        compiler_params=params(56),
        name="prepare",
    )(where, w_gate, w_up, w_down, ids, queries)


def to_rows_kernel(slabs, out):
    count = NZ * SLAB
    to, at = iota((count, count), 0), iota((count, count), 1)
    row = to // NZ
    row = jnp.where(row < 3 * CAP, row, row + 2)
    row = jnp.where(row >= SLAB - 2, SCALAR_ROW, row)
    select = ((to % NZ) * SLAB + row == at).astype(F32).astype(BF16)
    flat = slabs[...].reshape(count, LANES)
    out[...] = jnp.dot(select, flat, preferred_element_type=F32).astype(BF16)[: out.shape[0]]


def to_rows(slabs):
    return pl.pallas_call(
        to_rows_kernel,
        out_shape=jax.ShapeDtypeStruct((6 * ROWS + 16, LANES), BF16),
        in_specs=in_vmem(1),
        out_specs=in_vmem(1)[0],
        compiler_params=params(16),
        name="to_rows",
    )(slabs)


BLOCKS = [(c, g) for c in range(2) for g in range(2)]
PART_ROWS = 4 * ROWS + 4 * NZ


def gate_up_kernel(where, *refs):
    rows = (refs[0:4], refs[4:8])
    weights = refs[8:12]
    outs = refs[14:18]
    left = []
    for hm in range(2):
        for chunk in range(6):
            at = slice(chunk * ROWS, (chunk + 1) * ROWS)
            left.append(jnp.concatenate([rows[c][2 * hm + g][at, :] for c, g in BLOCKS], axis=0))
    left = [jnp.concatenate(left[6 * hm : 6 * hm + 6], axis=1) for hm in range(2)]
    scalars = []
    for hm in range(2):
        at = slice(6 * ROWS, 6 * ROWS + 16)
        scalars.append(
            jnp.concatenate([rows[c][2 * hm + g][at, :].astype(F32)[:NZ] for c, g in BLOCKS], axis=0)
        )
    scalars = jnp.concatenate(scalars, axis=1)
    for n in range(4):
        parts = []
        for hm in range(2):
            h = jnp.bitwise_xor(where[0], hm)
            at = pl.ds(pl.multiple_of(h * WIDTH, WIDTH), WIDTH)
            parts.append(jnp.dot(left[hm], weights[n][at, :], preferred_element_type=F32))
        total = parts[0] + parts[1]
        outs[n][: 4 * ROWS, :] = total.astype(outs[n].dtype)
        outs[n][4 * ROWS :, :] = scalars.astype(outs[n].dtype)


def gate_up(where, own, other, weights, later):
    out = jax.ShapeDtypeStruct((PART_ROWS, 2 * LANES), BF16)
    return pl.pallas_call(
        gate_up_kernel,
        out_shape=(jax.ShapeDtypeStruct(out.shape, F32), out, out, out),
        in_specs=in_smem(1) + in_vmem(12) + in_hbm(2),
        out_specs=tuple(in_vmem(4)),
        compiler_params=params(24),
        name="gate_up",
    )(where, *own, *other, *weights, *later)


def activate_kernel(*refs):
    outs = refs[4:6]
    for i, (c, g) in enumerate(BLOCKS):
        sums = jnp.zeros((NZ, 2 * LANES), F32)
        for ref in refs[:4]:
            sums = sums + ref[4 * ROWS :, :].astype(F32)[i * NZ : (i + 1) * NZ]
        sums = sums[:, :LANES] + sums[:, LANES:]

        def scalar(first):
            return sum(
                sums[:, (first + p) * CAP : (first + p + 1) * CAP] for p in range(PIECES)
            )

        inverse = lax.rsqrt(scalar(0) / (WIDTH * 8) + 1e-05)
        gate = 1.0 / (1.0 + jnp.exp(-scalar(PIECES) * inverse))
        at = slice(i * ROWS, (i + 1) * ROWS)
        part = (refs[0][at, :] + refs[1][at, :].astype(F32)) + (
            refs[2][at, :].astype(F32) + refs[3][at, :].astype(F32)
        )
        active = []
        for k in range(CAP):
            rows = part[k * NZ : (k + 1) * NZ] * inverse[:, k : k + 1]
            v, up = rows[:, :LANES], rows[:, LANES:]
            active.append(v / (1.0 + jnp.exp(-v)) * up * gate[:, k : k + 1])
        outs[g][c * ROWS : (c + 1) * ROWS, :] = jnp.concatenate(active, axis=0).astype(BF16)


def activate(parts):
    out = jax.ShapeDtypeStruct((2 * ROWS, LANES), BF16)
    return pl.pallas_call(
        activate_kernel,
        out_shape=(out, out),
        in_specs=in_vmem(4),
        out_specs=tuple(in_vmem(2)),
        compiler_params=params(8),
        name="activate",
    )(*parts)


def down_kernel(where, *refs):
    active, weights, outs = refs[0:4], refs[4:8], refs[8:10]
    left = jnp.concatenate([ref[...] for ref in active], axis=1)
    for n in range(4):
        x = jnp.bitwise_and(where[1] + n, 3)
        for pair in range(3):
            at = pl.ds(pl.multiple_of((x * 3 + pair) * LANES, LANES), LANES)
            right = jnp.concatenate([ref[at, :] for ref in weights], axis=0)
            made = jnp.dot(left, right, preferred_element_type=F32).astype(BF16)
            for c in range(2):
                for half in range(2):
                    chunk = 2 * pair + half
                    outs[c][n, chunk * ROWS : (chunk + 1) * ROWS, :] = made[
                        c * ROWS : (c + 1) * ROWS, half * LANES : (half + 1) * LANES
                    ]


def down(where, active, weights):
    out = jax.ShapeDtypeStruct((4, 6 * ROWS, LANES), BF16)
    return pl.pallas_call(
        down_kernel,
        out_shape=(out, out),
        in_specs=in_smem(1) + in_vmem(8),
        out_specs=tuple(in_vmem(2)),
        compiler_params=params(16),
        name="down",
    )(where, *active, *weights)


def add_cores_kernel(own, other, *outs):
    for m in range(4):
        outs[m][...] = (own[m].astype(F32) + other[m].astype(F32)).astype(BF16)


def add_cores(own, other):
    out = jax.ShapeDtypeStruct(own.shape[1:], BF16)
    return pl.pallas_call(
        add_cores_kernel,
        out_shape=(out,) * 4,
        in_specs=in_vmem(2),
        out_specs=tuple(in_vmem(4)),
        compiler_params=params(8),
        name="add_cores",
    )(own, other)


def to_slabs_kernel(*refs):
    count = NZ * SLAB
    summed = (refs[0][...].astype(F32) + refs[1][...].astype(F32)) + (
        refs[2][...].astype(F32) + refs[3][...].astype(F32)
    )
    to, at = iota((count, 6 * ROWS), 0), iota((count, 6 * ROWS), 1)
    row = jnp.where(at < 3 * ROWS, at // NZ, at // NZ + 2)
    select = ((at % NZ) * SLAB + row == to).astype(F32).astype(BF16)
    moved = jnp.dot(select, summed.astype(BF16), preferred_element_type=F32).astype(BF16)
    refs[4][...] = moved.reshape(NZ, SLAB, LANES)


def to_slabs(parts):
    return pl.pallas_call(
        to_slabs_kernel,
        out_shape=jax.ShapeDtypeStruct((NZ, SLAB, LANES), BF16),
        in_specs=in_vmem(4),
        out_specs=in_vmem(1)[0],
        compiler_params=params(8),
        name="to_slabs",
    )(*parts)


def combine_kernel(slabs, hidden, select, mixed):
    rows, width = hidden.shape
    total = jnp.zeros((LANES, LANES), F32)
    for half in range(2):
        flat = jnp.concatenate([slabs[NZ - 1 - 2 * e - half] for e in range(EXPERTS)], axis=0)
        total = total + lax.dot_general(
            select[...], flat, (((0,), (0,)), ((), ())), preferred_element_type=F32
        )
    blended = jnp.concatenate(
        [total[h * rows : (h + 1) * rows] for h in range(width // LANES)], axis=1
    )
    mixed[...] = (hidden[...].astype(F32) + blended).astype(BF16)


def combine(slabs, hidden, select):
    return pl.pallas_call(
        combine_kernel,
        out_shape=jax.ShapeDtypeStruct(hidden.shape, BF16),
        in_specs=in_vmem(3),
        out_specs=in_vmem(1)[0],
        compiler_params=params(16),
        name="combine",
    )(slabs, hidden, select)


def exchange_z(slabs):
    return lax.all_to_all(slabs, "attn", 0, 0, axis_index_groups=Z_GROUPS, tiled=True)


def on_device(
    queries,
    stream,
    kv_pool,
    fresh_kv,
    fresh_owner,
    page_table,
    lengths,
    norm_gain,
    router,
    expert_ids,
    w_gate,
    w_up,
    w_down,
):
    n_attn = lax.axis_size("attn")
    pages, kv_local, page_len, page_width = kv_pool.shape
    sect = lax.axis_index("sect")
    where = jnp.stack([sect // 4, sect % 4]).astype(jnp.int32)

    *blocks, select, places, heads = prepare(
        where, w_gate, w_up, w_down, expert_ids.T, queries
    )
    first = [blocks[0]] + [permute(blocks[n], along_x(n)) for n in (1, 2, 3)]
    second = [permute(blocks[4], along_y(1)), permute(blocks[5], along_y(3))]
    outgoing = pack_pages(fresh_owner.T, fresh_kv.reshape(-1, page_len, page_width), n_attn)
    arrived = lax.all_to_all(
        outgoing, "attn", 0, 0, axis_index_groups=PAGE_GROUPS, tiled=True
    )
    kv_out, hidden, payload = attend(
        page_table,
        lengths,
        kv_pool.reshape(pages, page_len, page_width),
        arrived,
        heads,
        stream,
        norm_gain.reshape(1, -1),
        router.T,
        select,
        places,
    )

    own = gather4(to_rows(exchange_z(payload)), along_y)
    other = [permute(v, OTHER_CORE) for v in own]
    parts = gate_up(where, own, other, first, second)
    far, *parts = lax.optimization_barrier((blocks[5], *parts))
    second = [blocks[4], second[0], permute(far, along_y(2)), second[1]]
    active = activate([parts[0]] + [permute(parts[n], along_x(-n)) for n in (1, 2, 3)])
    active = [active[0]] + [permute(active[m % 2], along_y(m)) for m in (1, 2, 3)]
    made, for_other = down(where, active, second)
    sums = add_cores(made, permute(for_other, OTHER_CORE))
    slabs = to_slabs([sums[0]] + [permute(sums[n], along_x(n)) for n in (1, 2, 3)])
    mixed = combine(exchange_z(slabs), hidden, select)
    return (mixed, kv_out.reshape(kv_pool.shape))


def solution(mesh):
    return jax.shard_map(
        on_device,
        mesh=mesh,
        in_specs=(
            P("attn", "sect"),
            P("attn", "sect"),
            P("attn", "sect", None, None),
            P("attn", "sect", None, None),
            P("attn", None),
            P("attn", None),
            P("attn", None),
            P("sect"),
            P("sect", None),
            P("attn", None),
            P(None, ("attn", "sect")),
            P(None, ("attn", "sect")),
            P(("attn", "sect"), None),
        ),
        out_specs=(P("attn", "sect"), P("attn", "sect", None, None)),
        check_vma=False,
    )
```

```python
import functools

import jax
import jax.numpy as jnp
from jax import lax
from jax.experimental import pallas as pl
from jax.experimental.pallas import tpu as pltpu
from jax.sharding import PartitionSpec as P

F32 = jnp.float32
BF16 = jnp.bfloat16
EXPERTS = 4
CAPP = 4
OLD_PAGES = 192
CAP = 10
WIDTH = 768
LANES = 128
SLAB = 64
SCALAR_ROW = 30
NZ = 8
ROWS = NZ * CAP
PIECES = 3
AXES = ("attn", "sect")
MIB = 1024 * 1024


def place(z, y, x, c):
    return (z * 4 + (y % 2) * 2 + c) * 8 + (y // 2) * 4 + x


def pairs(move):
    return [
        (place(z, y, x, c), place(*move(z, y, x, c)))
        for z in range(NZ)
        for y in range(4)
        for x in range(4)
        for c in range(2)
    ]


def along_x(step):
    return pairs(lambda z, y, x, c: (z, y, (x + step) % 4, c))


def along_y(step):
    return pairs(lambda z, y, x, c: (z, y ^ step, x, c))


OTHER_CORE = pairs(lambda z, y, x, c: (z, y, x, c ^ 1))
Z_GROUPS = [[z * 4 + r for z in reversed(range(NZ))] for r in range(4)]
PAGE_GROUPS = [[z * 4 + r for z in reversed(range(NZ)) for r in range(4)]]
OWNERS_Z = 4


def permute(value, perm):
    return lax.ppermute(value, AXES, perm)


def gather4(value, along):
    return [value] + [permute(value, along(step)) for step in (1, 2, 3)]


def in_vmem(count):
    return [pl.BlockSpec(memory_space=pltpu.VMEM)] * count


def in_hbm(count):
    return [pl.BlockSpec(memory_space=pltpu.HBM)] * count


def in_smem(count):
    return [pl.BlockSpec(memory_space=pltpu.SMEM)] * count


def params(mib):
    return pltpu.CompilerParams(vmem_limit_bytes=mib * MIB)


def iota(shape, dim):
    return lax.broadcasted_iota(jnp.int32, shape, dim)


def slab_offset(chunk):
    return jnp.where(chunk < 3, chunk * CAP, chunk * CAP + 2)


def pack_pages_kernel(owner, fresh, out, used):
    out[...] = jnp.zeros_like(out)

    def clear(o, carry):
        used[o] = 0
        return carry

    lax.fori_loop(0, used.shape[0], clear, 0)

    def put(p, carry):
        o = owner[0, p]
        k = used[o]
        at = (NZ - 1 - o // OWNERS_Z) * OWNERS_Z + o % OWNERS_Z
        out[at * CAPP + k] = fresh[p]
        used[o] = k + 1
        return carry

    lax.fori_loop(0, fresh.shape[0], put, 0, unroll=4)


def pack_pages(owners, fresh, n_attn):
    return pl.pallas_call(
        pack_pages_kernel,
        out_shape=jax.ShapeDtypeStruct((n_attn * CAPP,) + fresh.shape[1:], fresh.dtype),
        in_specs=in_smem(1) + in_vmem(1),
        out_specs=in_vmem(1)[0],
        scratch_shapes=[pltpu.SMEM((n_attn,), jnp.int32)],
        compiler_params=params(56),
        name="pack_pages",
    )(owners, fresh)


def split3(value):
    pieces = []
    for _ in range(PIECES):
        piece = value.astype(BF16).astype(F32)
        pieces.append(piece)
        value = value - piece
    return pieces


def find_places(ids, queries, select_out, places_out, heads_out):
    rows, width = queries.shape
    heads = width // LANES
    for h in range(heads):
        heads_out[pl.ds(h, rows, stride=8), :] = queries[:, h * LANES : (h + 1) * LANES].astype(F32)
    for h in range(heads, 8):
        heads_out[pl.ds(h, rows, stride=8), :] = jnp.zeros((rows, LANES), F32)
    ids_f = ids[...].astype(F32)
    cols = EXPERTS * 32
    spread = (iota((rows, cols), 1) % rows == iota((rows, cols), 0)).astype(F32)
    ids_l = jnp.dot(ids_f, spread, preferred_element_type=F32).astype(jnp.int32)
    e0, e1 = ids_l[0:1], ids_l[1:2]
    expert = iota((8, cols), 0)
    routed = ((expert == e0) | (expert == e1)).astype(F32)
    before = ((iota((cols, cols), 0) < rows) & (iota((cols, cols), 0) < iota((cols, cols), 1) % rows)).astype(F32)
    slot = jnp.dot(routed, before, preferred_element_type=F32).astype(jnp.int32)
    slot0 = jnp.sum(jnp.where(expert == e0, slot, 0), axis=0, keepdims=True)
    slot1 = jnp.sum(jnp.where(expert == e1, slot, 0), axis=0, keepdims=True)
    column = iota((1, cols), 1)
    offset = slab_offset(column // rows)
    features = column < heads * rows
    target0 = jnp.where(
        features,
        e0 * SLAB + slot0 + offset,
        jnp.where(column < (heads + 1) * rows, e0 * SLAB + SCALAR_ROW, -1),
    )
    target1 = jnp.where(
        features,
        e1 * SLAB + slot1 + offset,
        jnp.where(column < (heads + 1) * rows, -1, e1 * SLAB + SCALAR_ROW),
    )
    at = iota((EXPERTS * SLAB, cols), 0)
    select_out[...] = ((at == target0) | (at == target1)).astype(F32).astype(BF16)

    diagonal = (iota((rows, cols), 1) == iota((rows, cols), 0)).astype(F32)
    for i, value in enumerate((e0, e1, slot0, slot1)):
        column_of = jnp.sum(diagonal * value.astype(F32), axis=1, keepdims=True)
        places_out[i * rows : (i + 1) * rows, :] = jnp.broadcast_to(
            column_of.astype(jnp.int32), (rows, LANES)
        )


def attend_kernel(
    table,
    lengths,
    *refs,
):
    kv_pool, arrived, queries, ids = refs[:4]
    kv_out, hidden_out, payload, select = refs[7:11]
    pool, heads_v, stream, gain, router, places, scores_v, o_scr, sems = refs[11:]
    rows, width = stream.shape
    heads = width // LANES
    pages = table.shape[1]
    kept = pl.ds(0, OLD_PAGES)
    share = arrived.shape[0] // NZ
    loads = [
        pltpu.make_async_copy(source, target, sems.at[i])
        for i, (source, target) in enumerate(
            [
                (kv_pool.at[kept], pool.at[kept]),
                (refs[4], stream),
                (refs[5], gain),
                (refs[6], router),
            ]
        )
    ]
    for load in loads:
        load.start()
    for z in range(NZ):
        to, at = OLD_PAGES + z * share, (NZ - 1 - z) * share
        pool[to : to + share] = arrived[at : at + share]
    find_places(ids, queries, select, places, heads_v)
    loads[0].wait()
    store = pltpu.make_async_copy(pool, kv_out, sems.at[4])
    store.start()
    scale = float(LANES) ** (-0.5)
    length = jnp.concatenate(
        [jnp.full((8, 1), lengths[0, r], jnp.int32) for r in range(rows)], axis=0
    )
    for r in range(rows):
        keys = jnp.concatenate([pool[table[r, p], :, :LANES] for p in range(pages)], axis=0)
        query = heads_v[r * 8 : (r + 1) * 8, :]
        query = jnp.concatenate([query, query], axis=0).astype(BF16)
        scores = lax.dot_general(query, keys, (((1,), (1,)), ((), ())), preferred_element_type=F32)
        scores_v[r * 8 : (r + 1) * 8, :] = scores[:8]
    scores = scores_v[...] * scale
    valid = iota(scores.shape, 1) < length
    masked = jnp.where(valid, scores, -1e30)
    top = jnp.max(masked, axis=1, keepdims=True)
    weights = jnp.where(valid, jnp.exp(masked - top), 0.0)
    total = jnp.sum(weights, axis=1, keepdims=True)
    scores_v[...] = weights
    for r in range(rows):
        values = jnp.concatenate([pool[table[r, p], :, LANES:] for p in range(pages)], axis=0)
        weight = scores_v[r * 8 : (r + 1) * 8, :]
        weight = jnp.concatenate([weight, weight], axis=0).astype(BF16)
        o_scr[r * 8 : (r + 1) * 8, :] = jnp.dot(weight, values, preferred_element_type=F32)[:8]
    o_scr[...] = o_scr[...] / total
    for load in loads[1:]:
        load.wait()
    attended = jnp.concatenate([o_scr[pl.ds(h, rows, stride=8), :] for h in range(heads)], axis=1)
    hidden = (stream[...].astype(F32) + attended).astype(BF16)
    hidden_out[...] = hidden
    hidden_f = hidden.astype(F32)
    squares = jnp.sum(hidden_f * hidden_f, axis=1, keepdims=True)
    gained = (hidden_f * gain[...].astype(F32)).astype(BF16)
    logits = lax.dot_general(gained, router[...], (((1,), (1,)), ((), ())), preferred_element_type=F32)
    expert_r = iota(logits.shape, 1)
    c0, c1, slot_c0, slot_c1 = [places[i * rows : (i + 1) * rows, :] for i in range(4)]
    delta = jnp.sum(
        jnp.where(expert_r == c0[:, :EXPERTS], logits, 0.0)
        - jnp.where(expert_r == c1[:, :EXPERTS], logits, 0.0),
        axis=1,
        keepdims=True,
    )
    lane = iota((rows, LANES), 1)

    def scalars(slots, difference):
        total = jnp.zeros((rows, LANES), F32)
        for i, piece in enumerate(split3(squares) + split3(difference)):
            total = total + jnp.where(lane == i * CAP + slots, piece, 0.0)
        return total.astype(BF16)

    parts = [gained[:, h * LANES : (h + 1) * LANES] for h in range(heads)]
    parts += [scalars(slot_c0, delta), scalars(slot_c1, -delta)]
    stacked = jnp.concatenate(parts, axis=0)
    slabs = jnp.dot(select[...], stacked, preferred_element_type=F32).astype(BF16)
    for e in range(EXPERTS):
        slab = slabs[e * SLAB : (e + 1) * SLAB]
        payload[NZ - 1 - 2 * e] = slab
        payload[NZ - 2 - 2 * e] = slab
    store.wait()


def attend(table, lengths, kv_pool, arrived, queries, ids, stream, gain, router):
    rows, width = stream.shape
    shape = jax.ShapeDtypeStruct
    return pl.pallas_call(
        attend_kernel,
        out_shape=(
            shape(kv_pool.shape, kv_pool.dtype),
            shape((rows, width), BF16),
            shape((NZ, SLAB, LANES), BF16),
            shape((EXPERTS * SLAB, LANES), BF16),
        ),
        in_specs=in_smem(2) + in_hbm(1) + in_vmem(3) + in_hbm(3),
        out_specs=tuple(in_hbm(1) + in_vmem(3)),
        scratch_shapes=[
            pltpu.VMEM(kv_pool.shape, kv_pool.dtype),
            pltpu.VMEM((rows * 8, LANES), F32),
            pltpu.VMEM(stream.shape, BF16),
            pltpu.VMEM(gain.shape, BF16),
            pltpu.VMEM(router.shape, BF16),
            pltpu.VMEM((4 * rows, LANES), jnp.int32),
            pltpu.VMEM((rows * 8, table.shape[1] * kv_pool.shape[1]), F32),
            pltpu.VMEM((rows * 8, LANES), F32),
            pltpu.SemaphoreType.DMA((5,)),
        ],
        compiler_params=params(53),
        name="attend",
    )(table, lengths, kv_pool, arrived, queries, ids, stream, gain, router)


def prepare_kernel(where, w_gate, w_up, w_down, *refs):
    made, blocks, sems = refs[:6], refs[6:12], refs[12]
    pieces = []
    for n in range(4):
        x = jnp.bitwise_and(where[1] + n, 3)
        for h in range(2):
            at = pl.ds(pl.multiple_of((h * 4 + x) * WIDTH, WIDTH), WIDTH)
            to = pl.ds(h * WIDTH, WIDTH)
            pieces.append((n, w_gate.at[at, :], blocks[n].at[to, pl.ds(0, LANES)]))
            pieces.append((n, w_up.at[at, :], blocks[n].at[to, pl.ds(LANES, LANES)]))
    for hm in range(2):
        h = jnp.bitwise_xor(where[0], hm)
        for pair in range(12):
            start = pl.multiple_of(h * 4 * WIDTH + pair * 2 * LANES, 2 * LANES)
            to = pl.ds(pair * LANES, LANES)
            pieces.append((4 + hm, w_down.at[:, pl.ds(start, 2 * LANES)], blocks[4 + hm].at[to, :]))
    loads = [
        (n, pltpu.make_async_copy(source, target, sems.at[i]))
        for i, (n, source, target) in enumerate(pieces)
    ]
    for _, load in loads:
        load.start()
    stores = []
    for n in range(6):
        for block, load in loads:
            if block == n:
                load.wait()
        stores.append(pltpu.make_async_copy(blocks[n], made[n], sems.at[40 + n]))
        stores[n].start()
    for store in stores:
        store.wait()


def prepare(where, w_gate, w_up, w_down):
    block = (2 * WIDTH, 2 * LANES)
    shape = jax.ShapeDtypeStruct
    return pl.pallas_call(
        prepare_kernel,
        out_shape=(shape(block, BF16),) * 6,
        in_specs=in_smem(1) + in_hbm(3),
        out_specs=tuple(in_hbm(6)),
        scratch_shapes=[pltpu.VMEM(block, BF16)] * 6 + [pltpu.SemaphoreType.DMA((46,))],
        compiler_params=params(56),
        name="prepare",
    )(where, w_gate, w_up, w_down)


def to_rows_kernel(slabs, out):
    count = NZ * SLAB
    to, at = iota((count, count), 0), iota((count, count), 1)
    row = to // NZ
    row = jnp.where(row < 3 * CAP, row, row + 2)
    row = jnp.where(row >= SLAB - 2, SCALAR_ROW, row)
    select = ((to % NZ) * SLAB + row == at).astype(F32).astype(BF16)
    flat = slabs[...].reshape(count, LANES)
    out[...] = jnp.dot(select, flat, preferred_element_type=F32).astype(BF16)[: out.shape[0]]


def to_rows(slabs):
    return pl.pallas_call(
        to_rows_kernel,
        out_shape=jax.ShapeDtypeStruct((6 * ROWS + 16, LANES), BF16),
        in_specs=in_vmem(1),
        out_specs=in_vmem(1)[0],
        compiler_params=params(16),
        name="to_rows",
    )(slabs)


BLOCKS = [(c, g) for c in range(2) for g in range(2)]
PART_ROWS = 4 * ROWS + 4 * NZ


def gate_up_kernel(where, *refs):
    rows = (refs[0:4], refs[4:8])
    weights = refs[8:12]
    outs = refs[14:18]
    left = []
    for hm in range(2):
        for chunk in range(6):
            at = slice(chunk * ROWS, (chunk + 1) * ROWS)
            left.append(jnp.concatenate([rows[c][2 * hm + g][at, :] for c, g in BLOCKS], axis=0))
    left = [jnp.concatenate(left[6 * hm : 6 * hm + 6], axis=1) for hm in range(2)]
    scalars = []
    for hm in range(2):
        at = slice(6 * ROWS, 6 * ROWS + 16)
        scalars.append(
            jnp.concatenate([rows[c][2 * hm + g][at, :].astype(F32)[:NZ] for c, g in BLOCKS], axis=0)
        )
    scalars = jnp.concatenate(scalars, axis=1)
    for n in range(4):
        parts = []
        for hm in range(2):
            h = jnp.bitwise_xor(where[0], hm)
            at = pl.ds(pl.multiple_of(h * WIDTH, WIDTH), WIDTH)
            parts.append(jnp.dot(left[hm], weights[n][at, :], preferred_element_type=F32))
        total = parts[0] + parts[1]
        outs[n][: 4 * ROWS, :] = total.astype(outs[n].dtype)
        outs[n][4 * ROWS :, :] = scalars.astype(outs[n].dtype)


def gate_up(where, own, other, weights, later):
    out = jax.ShapeDtypeStruct((PART_ROWS, 2 * LANES), BF16)
    return pl.pallas_call(
        gate_up_kernel,
        out_shape=(jax.ShapeDtypeStruct(out.shape, F32), out, out, out),
        in_specs=in_smem(1) + in_vmem(12) + in_hbm(2),
        out_specs=tuple(in_vmem(4)),
        compiler_params=params(24),
        name="gate_up",
    )(where, *own, *other, *weights, *later)


def activate_kernel(*refs):
    outs = refs[4:6]
    for i, (c, g) in enumerate(BLOCKS):
        sums = jnp.zeros((NZ, 2 * LANES), F32)
        for ref in refs[:4]:
            sums = sums + ref[4 * ROWS :, :].astype(F32)[i * NZ : (i + 1) * NZ]
        sums = sums[:, :LANES] + sums[:, LANES:]

        def scalar(first):
            return sum(
                sums[:, (first + p) * CAP : (first + p + 1) * CAP] for p in range(PIECES)
            )

        inverse = lax.rsqrt(scalar(0) / (WIDTH * 8) + 1e-05)
        gate = 1.0 / (1.0 + jnp.exp(-scalar(PIECES) * inverse))
        at = slice(i * ROWS, (i + 1) * ROWS)
        part = (refs[0][at, :] + refs[1][at, :].astype(F32)) + (
            refs[2][at, :].astype(F32) + refs[3][at, :].astype(F32)
        )
        active = []
        for k in range(CAP):
            rows = part[k * NZ : (k + 1) * NZ] * inverse[:, k : k + 1]
            v, up = rows[:, :LANES], rows[:, LANES:]
            active.append(v / (1.0 + jnp.exp(-v)) * up * gate[:, k : k + 1])
        outs[g][c * ROWS : (c + 1) * ROWS, :] = jnp.concatenate(active, axis=0).astype(BF16)


def activate(parts):
    out = jax.ShapeDtypeStruct((2 * ROWS, LANES), BF16)
    return pl.pallas_call(
        activate_kernel,
        out_shape=(out, out),
        in_specs=in_vmem(4),
        out_specs=tuple(in_vmem(2)),
        compiler_params=params(8),
        name="activate",
    )(*parts)


def down_kernel(where, *refs):
    active, weights, outs = refs[0:4], refs[4:8], refs[8:10]
    left = jnp.concatenate([ref[...] for ref in active], axis=1)
    for n in range(4):
        x = jnp.bitwise_and(where[1] + n, 3)
        for pair in range(3):
            at = pl.ds(pl.multiple_of((x * 3 + pair) * LANES, LANES), LANES)
            right = jnp.concatenate([ref[at, :] for ref in weights], axis=0)
            made = jnp.dot(left, right, preferred_element_type=F32).astype(BF16)
            for c in range(2):
                for half in range(2):
                    chunk = 2 * pair + half
                    outs[c][n, chunk * ROWS : (chunk + 1) * ROWS, :] = made[
                        c * ROWS : (c + 1) * ROWS, half * LANES : (half + 1) * LANES
                    ]


def down(where, active, weights):
    out = jax.ShapeDtypeStruct((4, 6 * ROWS, LANES), BF16)
    return pl.pallas_call(
        down_kernel,
        out_shape=(out, out),
        in_specs=in_smem(1) + in_vmem(8),
        out_specs=tuple(in_vmem(2)),
        compiler_params=params(16),
        name="down",
    )(where, *active, *weights)


def add_cores_kernel(own, other, *outs):
    for m in range(4):
        outs[m][...] = (own[m].astype(F32) + other[m].astype(F32)).astype(BF16)


def add_cores(own, other):
    out = jax.ShapeDtypeStruct(own.shape[1:], BF16)
    return pl.pallas_call(
        add_cores_kernel,
        out_shape=(out,) * 4,
        in_specs=in_vmem(2),
        out_specs=tuple(in_vmem(4)),
        compiler_params=params(8),
        name="add_cores",
    )(own, other)


def to_slabs_kernel(*refs):
    count = NZ * SLAB
    summed = (refs[0][...].astype(F32) + refs[1][...].astype(F32)) + (
        refs[2][...].astype(F32) + refs[3][...].astype(F32)
    )
    to, at = iota((count, 6 * ROWS), 0), iota((count, 6 * ROWS), 1)
    row = jnp.where(at < 3 * ROWS, at // NZ, at // NZ + 2)
    select = ((at % NZ) * SLAB + row == to).astype(F32).astype(BF16)
    moved = jnp.dot(select, summed.astype(BF16), preferred_element_type=F32).astype(BF16)
    refs[4][...] = moved.reshape(NZ, SLAB, LANES)


def to_slabs(parts):
    return pl.pallas_call(
        to_slabs_kernel,
        out_shape=jax.ShapeDtypeStruct((NZ, SLAB, LANES), BF16),
        in_specs=in_vmem(4),
        out_specs=in_vmem(1)[0],
        compiler_params=params(8),
        name="to_slabs",
    )(*parts)


def combine_kernel(slabs, hidden, select, mixed):
    rows, width = hidden.shape
    total = jnp.zeros((LANES, LANES), F32)
    for half in range(2):
        flat = jnp.concatenate([slabs[NZ - 1 - 2 * e - half] for e in range(EXPERTS)], axis=0)
        total = total + lax.dot_general(
            select[...], flat, (((0,), (0,)), ((), ())), preferred_element_type=F32
        )
    blended = jnp.concatenate(
        [total[h * rows : (h + 1) * rows] for h in range(width // LANES)], axis=1
    )
    mixed[...] = (hidden[...].astype(F32) + blended).astype(BF16)


def combine(slabs, hidden, select):
    return pl.pallas_call(
        combine_kernel,
        out_shape=jax.ShapeDtypeStruct(hidden.shape, BF16),
        in_specs=in_vmem(3),
        out_specs=in_vmem(1)[0],
        compiler_params=params(16),
        name="combine",
    )(slabs, hidden, select)


def exchange_z(slabs):
    return lax.all_to_all(slabs, "attn", 0, 0, axis_index_groups=Z_GROUPS, tiled=True)


def on_device(
    queries,
    stream,
    kv_pool,
    fresh_kv,
    fresh_owner,
    page_table,
    lengths,
    norm_gain,
    router,
    expert_ids,
    w_gate,
    w_up,
    w_down,
):
    n_attn = lax.axis_size("attn")
    pages, kv_local, page_len, page_width = kv_pool.shape
    sect = lax.axis_index("sect")
    where = jnp.stack([sect // 4, sect % 4]).astype(jnp.int32)

    blocks = prepare(where, w_gate, w_up, w_down)
    first = [blocks[0]] + [permute(blocks[n], along_x(n)) for n in (1, 2, 3)]
    second = [permute(blocks[4], along_y(1)), permute(blocks[5], along_y(3))]
    outgoing = pack_pages(fresh_owner.T, fresh_kv.reshape(-1, page_len, page_width), n_attn)
    arrived = lax.all_to_all(
        outgoing, "attn", 0, 0, axis_index_groups=PAGE_GROUPS, tiled=True
    )
    kv_out, hidden, payload, select = attend(
        page_table,
        lengths,
        kv_pool.reshape(pages, page_len, page_width),
        arrived,
        queries,
        expert_ids.T,
        stream,
        norm_gain.reshape(1, -1),
        router.T,
    )

    own = gather4(to_rows(exchange_z(payload)), along_y)
    other = [permute(v, OTHER_CORE) for v in own]
    parts = gate_up(where, own, other, first, second)
    far, *parts = lax.optimization_barrier((blocks[5], *parts))
    second = [blocks[4], second[0], permute(far, along_y(2)), second[1]]
    active = activate([parts[0]] + [permute(parts[n], along_x(-n)) for n in (1, 2, 3)])
    active = [active[0]] + [permute(active[m % 2], along_y(m)) for m in (1, 2, 3)]
    made, for_other = down(where, active, second)
    sums = add_cores(made, permute(for_other, OTHER_CORE))
    slabs = to_slabs([sums[0]] + [permute(sums[n], along_x(n)) for n in (1, 2, 3)])
    mixed = combine(exchange_z(slabs), hidden, select)
    return (mixed, kv_out.reshape(kv_pool.shape))


def solution(mesh):
    return jax.shard_map(
        on_device,
        mesh=mesh,
        in_specs=(
            P("attn", "sect"),
            P("attn", "sect"),
            P("attn", "sect", None, None),
            P("attn", "sect", None, None),
            P("attn", None),
            P("attn", None),
            P("attn", None),
            P("sect"),
            P("sect", None),
            P("attn", None),
            P(None, ("attn", "sect")),
            P(None, ("attn", "sect")),
            P(("attn", "sect"), None),
        ),
        out_specs=(P("attn", "sect"), P("attn", "sect", None, None)),
        check_vma=False,
    )
```
